512 devices in a mesh: row: 16 (over z_lo, x), col: 32 (over z_hi, y, core).
Axes of the slice: x: 4, y: 8, z: 8 (z_hi: 2, z_lo: 4; z = z_hi * 4 + z_lo), core: 2. Of those that a mesh axis runs over, the one named last changes fastest.
Arguments:
- features: bfloat16 [65536, 256], P(('col', 'row')), may hold values from -6 to 6
- weight: bfloat16 [256, 256], replicated, may hold values from -0.375 to 0.375
- cotangent: bfloat16 [65536, 256], P(('row', 'col')), may hold values from -6 to 6
- blocks: bfloat16 [16, 32, 96, 128, 128], P('row', 'col'), may hold values from -0.078125 to 0.078125
- block_pos: int32 [16, 32, 96], P('row', 'col'), may hold values from 0 to 511, as said below
- counts: int32 [16, 32], P('row', 'col'), may hold values from 1 to 96, as said below
Outputs:
- output: bfloat16 [65536, 256], P(('row', 'col'))
- input_grad: bfloat16 [65536, 256], P(('col', 'row'))
- weight_grad: float32 [256, 256], replicated
The draws below stay inside these ranges and needn't reach their ends.
Inputs may be any that keep to these rules, and one draw needn't show every extreme that they name: `block_pos`: within one tile the first counts[r, c] slots name distinct positions; the later slots carry no block. `counts`: some tile lists all 96 slots in every draw; loads differ widely between tiles.
All inputs are finite; a program needn't handle non-finite values.
Results may differ from the reference program's by a relative error of at most 0.029.
Values may be sent and summed in bfloat16 or wider, within the bound.
No kernel may reach another device: no remote copies, remote signals or barrier semaphores. Data moves between devices by JAX's collectives and lax.ppermute only.
A program may use at most 128 MiB of HBM per device.

```python
import jax
import jax.numpy as jnp
from jax import lax

F = 256
BS = 128
TILE_DEG = 3
TBR = 32
TBC = 16
MAXB = 96
NODES = 65536
N_ROW = 16
N_COL = 32


def tile_choice(key):
    return jax.random.permutation(key, TBR * TBC)[:MAXB]


def draw_block_pos(key, part):
    key = jax.random.fold_in(key, 11)
    keys = jax.random.split(key, N_ROW * N_COL)
    picks = jax.vmap(tile_choice)(keys)
    return picks.reshape(N_ROW, N_COL, MAXB).astype(jnp.int32)


def draw_counts(key, part):
    key = jax.random.fold_in(key, 23)
    first, second, third = jax.random.split(key, 3)
    light = jax.random.randint(first, (N_ROW, N_COL), max(MAXB // 8, 1), MAXB // 2 + 1)
    heavy = jax.random.randint(second, (N_ROW, N_COL), 0, 8) == 0
    chosen = jax.random.randint(third, (), 0, N_ROW * N_COL)
    flat_index = jnp.arange(N_ROW * N_COL, dtype=jnp.int32).reshape(N_ROW, N_COL)
    return jnp.where(heavy | (flat_index == chosen), MAXB, light).astype(jnp.int32)


def levels(stream_key, extent, shards, low, high):
    level, own = 1.0, jax.random.fold_in(stream_key, 6)
    for dim, parts in shards:
        draws = jnp.exp(jax.random.uniform(jax.random.fold_in(own, dim), (parts,), jnp.float32, low / len(shards), high / len(shards)))
        level = level * jnp.repeat(draws, extent[dim] // parts).reshape([-1 if axis == dim else 1 for axis in range(len(extent))])
    return level


def bell_draw(stream_key, shape, scale, bound, cuts=(), kind=jnp.bfloat16):
    entries = scale * jax.random.normal(stream_key, shape, jnp.float32)
    if cuts:
        entries = entries * levels(stream_key, shape, cuts, -0.22, 0.18)
    return jnp.clip(entries, -bound, bound).astype(kind)


def setup_inputs(seed: int = 0) -> dict:
    streams_of = jax.random.split(jax.random.key(seed), 7)
    features = bell_draw(streams_of[0], (NODES, F), 1.0, 6.0, ((0, 512),))
    weight = bell_draw(streams_of[1], (F, F), F ** -0.5, 0.375)
    cotangent = bell_draw(streams_of[2], (NODES, F), 1.0, 6.0, ((0, 512),))
    blocks = bell_draw(streams_of[3], (N_ROW, N_COL, MAXB, BS, BS), (TILE_DEG * BS * N_COL // 2) ** -0.5, 0.078125, ((0, 16), (1, 32)))
    block_pos = draw_block_pos(jax.random.fold_in(streams_of[6], 71), 0)
    counts = draw_counts(jax.random.fold_in(streams_of[6], 71), 0)
    return {"features": features, "weight": weight, "cotangent": cotangent, "blocks": blocks, "block_pos": block_pos, "counts": counts}


def slope_of(pre):
    sigma = jax.nn.sigmoid(pre)
    return sigma * (1.0 + pre * (1.0 - sigma))


def forward_tile(tile, place, count, source):
    width = source.shape[-1]
    target = place // TBC
    anchor = place % TBC
    valid = jnp.arange(MAXB, dtype=jnp.int32) < count
    picked = jnp.take(source, anchor, axis=0)
    products = jnp.einsum('kij,kjf->kif', tile.astype(jnp.float32), picked)
    members = jnp.where((target[None, :] == jnp.arange(TBR, dtype=jnp.int32)[:, None]) & valid[None, :], 1.0, 0.0).astype(jnp.float32)
    summed = jnp.einsum('bk,kif->bif', members, products, precision=lax.Precision.HIGHEST)
    return summed.reshape(TBR * BS, width)


def backward_tile(tile, place, count, source):
    width = source.shape[-1]
    target = place // TBC
    anchor = place % TBC
    valid = jnp.arange(MAXB, dtype=jnp.int32) < count
    picked = jnp.take(source, target, axis=0)
    products = jnp.einsum('kji,kjf->kif', tile.astype(jnp.float32), picked)
    members = jnp.where((anchor[None, :] == jnp.arange(TBC, dtype=jnp.int32)[:, None]) & valid[None, :], 1.0, 0.0).astype(jnp.float32)
    summed = jnp.einsum('bk,kif->bif', members, products, precision=lax.Precision.HIGHEST)
    return summed.reshape(TBC * BS, width)


def reference(features, weight, cotangent, blocks, block_pos, counts):
    width = features.shape[1]
    source = features.astype(jnp.float32).reshape(N_COL, TBC, BS, width)

    def row_group(r):
        def add_part(total, c):
            part = forward_tile(blocks[r, c], block_pos[r, c], counts[r, c], source[c])
            part = lax.optimization_barrier(part.astype(jnp.bfloat16)).astype(jnp.float32)
            return total + part, None
        total, _ = lax.scan(add_part, jnp.zeros((TBR * BS, width), jnp.float32), jnp.arange(N_COL, dtype=jnp.int32))
        return total

    summed = lax.map(row_group, jnp.arange(N_ROW, dtype=jnp.int32)).reshape(NODES, width)
    aggregated = summed.astype(jnp.bfloat16)
    pre = jnp.dot(aggregated, weight, preferred_element_type=jnp.float32)
    output = jax.nn.silu(pre).astype(jnp.bfloat16)
    slopes = (cotangent.astype(jnp.float32) * slope_of(pre)).astype(jnp.bfloat16)
    weight_grad = lax.dot_general(aggregated, slopes, (((0,), (0,)), ((), ())), preferred_element_type=jnp.float32) * (NODES ** -0.5)
    grouped = slopes.astype(jnp.float32).reshape(N_ROW, TBR, BS, width)

    def col_group(c):
        def add_part(total, r):
            return total + backward_tile(blocks[r, c], block_pos[r, c], counts[r, c], grouped[r]), None
        total, _ = lax.scan(add_part, jnp.zeros((TBC * BS, width), jnp.float32), jnp.arange(N_ROW, dtype=jnp.int32))
        return total

    back = lax.map(col_group, jnp.arange(N_COL, dtype=jnp.int32)).reshape(NODES, width)
    input_grad = jnp.dot(back.astype(jnp.bfloat16), weight.T, preferred_element_type=jnp.float32).astype(jnp.bfloat16)
    return (output, input_grad, weight_grad)
```

```python
import functools
import math

import jax
import jax.numpy as jnp
from jax import lax
from jax.experimental import pallas as pl
from jax.experimental.pallas import tpu as pltpu
from jax.sharding import Mesh
from jax.sharding import PartitionSpec as P

BF = jnp.bfloat16
F32 = jnp.float32
GROUP = 4
VMEM = pl.BlockSpec(memory_space=pltpu.VMEM)
SMEM = pl.BlockSpec(memory_space=pltpu.SMEM)
LIMIT = pltpu.CompilerParams(vmem_limit_bytes=48 * 1024 * 1024)


def dot(a, b, dims=(((1,), (0,)), ((), ()))):
    return lax.dot_general(a, b, dims, preferred_element_type=F32)


def forward_kernel(place, info, blocks, nodes, keep, send, acc):
    acc[...] = jnp.zeros_like(acc)
    count, core = info[0], info[1]

    def step(i, _):
        products = []
        for g in range(GROUP):
            k = i * GROUP + g
            p = place[k]
            t, a = p // 16, p % 16
            source = nodes[(a % 4) * 4 + a // 4]
            slot = ((t % 2) ^ core) * 16 + t // 2
            products.append((jnp.where(k < count, slot, 32), dot(blocks[k], source)))
        for slot, product in products:
            acc[slot] += product
        return 0

    lax.fori_loop(0, pl.cdiv(count, GROUP), step, 0)
    keep[...] = acc[0:16].astype(BF)
    send[...] = acc[16:32].astype(BF)


def middle_kernel(parts, weight, cotangent, output, spread):
    total = parts[0].astype(F32)
    for s in range(1, 16):
        total += parts[s].astype(F32)
    share = total.astype(BF)
    pre = dot(share, weight[...])
    sigma = 1.0 / (1.0 + jnp.exp(-pre))
    output[...] = (pre * sigma).astype(BF)
    slope = sigma * (1.0 + pre * (1.0 - sigma))
    slopes32 = cotangent[...].astype(F32) * slope
    slopes = slopes32.astype(BF)
    turned = slopes.astype(F32).T.astype(BF)
    grad = dot(share.astype(F32).T.astype(BF), slopes).astype(BF)
    for s in range(16):
        spread[s, 0:256, :] = turned
        spread[s, 256:272, :] = grad[16 * s : 16 * s + 16, 0:128]
        spread[s, 272:288, :] = grad[16 * s : 16 * s + 16, 128:256]


def split(value):
    high = value.astype(BF)
    return high, (value - high.astype(F32)).astype(BF)


def backward_kernel(place, info, blocks, own, other, out, acc):
    acc[...] = jnp.zeros_like(acc)
    count, core = info[0], info[1]

    def step(i, _):
        products = []
        for g in range(GROUP):
            k = i * GROUP + g
            p = place[k]
            t, a = p // 16, p % 16
            h = t // 2
            source = jnp.where(t % 2 == core, own[h, 0:256, :], other[h, 0:256, :])
            slot = (a % 4) * 4 + a // 4
            products.append((jnp.where(k < count, slot, 16), dot(source, blocks[k])))
        for slot, product in products:
            acc[slot] += product
        return 0

    lax.fori_loop(0, pl.cdiv(count, GROUP), step, 0)
    grad = jnp.zeros((32, 128), F32)
    for s in range(16):
        grad += own[s, 256:288, :].astype(F32) + other[s, 256:288, :].astype(F32)
    high, low = split(grad)
    for x in range(4):
        for z in range(4):
            out[x, 256 * z : 256 * z + 256, :] = acc[4 * x + z].astype(BF)
        out[x, 1024:1056, :] = high
        out[x, 1056:1088, :] = low


def fold_kernel(parts, out):
    for z in range(4):
        rows = slice(256 * z, 256 * z + 256)
        total = parts[0, rows, :].astype(F32)
        for x in range(1, 4):
            total += parts[x, rows, :].astype(F32)
        out[z, 0:256, :] = total.astype(BF)
    grad = jnp.zeros((32, 128), F32)
    for x in range(4):
        grad += parts[x, 1024:1056, :].astype(F32) + parts[x, 1056:1088, :].astype(F32)
    high, low = split(grad)
    for z in range(4):
        out[z, 256:288, :] = high
        out[z, 288:320, :] = low


def last_kernel(scale, parts, weight, input_grad, grad_out):
    total = parts[0, 0:256, :].astype(F32)
    for z in range(1, 4):
        total += parts[z, 0:256, :].astype(F32)
    back = total.astype(BF).astype(F32).T.astype(BF)
    input_grad[...] = dot(back, weight[...], (((1,), (1,)), ((), ()))).astype(BF)
    grad = jnp.zeros((32, 128), F32)
    for z in range(4):
        grad += parts[z, 256:288, :].astype(F32) + parts[z, 288:320, :].astype(F32)
    grad = grad * scale
    for s in range(16):
        grad_out[s, :, 0:128] = grad[0:16]
        grad_out[s, :, 128:256] = grad[16:32]


def call(kernel, shapes, kinds, scratch=(), flops=0, size=0):
    return pl.pallas_call(
        kernel,
        out_shape=[jax.ShapeDtypeStruct(s, d) for s, d in shapes],
        in_specs=kinds,
        out_specs=[VMEM] * len(shapes),
        scratch_shapes=list(scratch),
        compiler_params=LIMIT,
        cost_estimate=pl.CostEstimate(flops=flops, bytes_accessed=size, transcendentals=0),
    )


def exchange(value, axes):
    return lax.all_to_all(value, axes, 0, 0, tiled=True)


def swap(value):
    return lax.ppermute(value, "c", [(0, 1), (1, 0)])


def shards(features, weight, cotangent, blocks, block_pos, counts):
    tile = blocks[0, 0]
    place = block_pos[0, 0]
    info = jnp.stack([counts[0, 0], lax.axis_index("c").astype(jnp.int32)])
    nodes_total = 65536

    lines = exchange(jnp.broadcast_to(features[None], (4, 128, 256)), "zl")
    nodes = exchange(jnp.broadcast_to(lines[None], (4, 4, 128, 256)), "x").reshape(16, 128, 256)
    keep, send = call(
        forward_kernel,
        [((16, 128, 256), BF)] * 2,
        [SMEM, SMEM, VMEM, VMEM],
        [pltpu.VMEM((33, 128, 256), F32)],
        flops=8 * 10**8,
        size=6 * 2**20,
    )(place, info, tile, nodes)
    pair = (keep.astype(F32) + swap(send).astype(F32)).astype(BF)
    parts = exchange(pair, ("zh", "y"))
    output, spread = call(
        middle_kernel,
        [((128, 256), BF), ((16, 288, 128), BF)],
        [VMEM, VMEM, VMEM],
    )(parts, weight, cotangent)
    own = exchange(spread, ("zh", "y"))
    other = swap(own)
    (back,) = call(
        backward_kernel,
        [((4, 1088, 128), BF)],
        [SMEM, SMEM, VMEM, VMEM, VMEM],
        [pltpu.VMEM((17, 256, 128), F32)],
        flops=8 * 10**8,
        size=6 * 2**20,
    )(place, info, tile, own, other)
    (folded,) = call(fold_kernel, [((4, 320, 128), BF)], [VMEM])(exchange(back, "x"))
    input_grad, grad = call(
        functools.partial(last_kernel, 1.0 / math.sqrt(nodes_total)),
        [((128, 256), BF), ((16, 16, 256), F32)],
        [VMEM, VMEM],
    )(exchange(folded, "zl"), weight)
    weight_grad = exchange(grad, ("zh", "y")).reshape(256, 256)
    return (output, input_grad, weight_grad)


def solution(mesh):
    names = ("zl", "x", "zh", "y", "c")
    row, col = names[:2], names[2:]
    fine = Mesh(mesh.devices.reshape(4, 4, 2, 8, 2), names)
    return jax.shard_map(
        shards,
        mesh=fine,
        in_specs=(
            P(col + row, None),
            P(),
            P(row + col, None),
            P(row, col, None, None, None),
            P(row, col, None),
            P(row, col),
        ),
        out_specs=(P(row + col, None), P(col + row, None), P()),
        check_vma=False,
    )
```

```python
import functools
import math

import jax
import jax.numpy as jnp
from jax import lax
from jax.experimental import pallas as pl
from jax.experimental.pallas import tpu as pltpu
from jax.sharding import Mesh
from jax.sharding import PartitionSpec as P

BF = jnp.bfloat16
F32 = jnp.float32
GROUP = 16
SLOTS = 112
VMEM = pl.BlockSpec(memory_space=pltpu.VMEM)
SMEM = pl.BlockSpec(memory_space=pltpu.SMEM)
LIMIT = pltpu.CompilerParams(vmem_limit_bytes=48 * 1024 * 1024)


def dot(a, b, dims=(((1,), (0,)), ((), ()))):
    return lax.dot_general(a, b, dims, preferred_element_type=F32)


def plan_kernel(place, info, lists, groups):
    count, core, xi, zi = info[0], info[1], info[2], info[3]

    def write(at, k, t, source, half, target):
        for f, value in enumerate((k, t, source, half, target)):
            lists[f * 2 * SLOTS + at] = value

    def step(k, held):
        p = place[k]
        t, a = p >> 4, p & 15
        z, x = a >> 2, a & 3
        half = t >> 1
        source = (((xi - x) & 3) << 2) + ((zi - z) & 3)
        target = (((x - xi) & 3) << 2) + ((z - zi) & 3)
        mine, theirs = held
        away = (t & 1) ^ core
        write(jnp.where(away == 0, mine, SLOTS + theirs), k, half, source, half, target)
        return mine + 1 - away, theirs + away

    mine, theirs = lax.fori_loop(0, count, step, (jnp.int32(0), jnp.int32(0)))
    for i, n in enumerate((mine, theirs)):
        for g in range(GROUP):
            write(i * SLOTS + n + g, 0, 16, 0, 0, 16)
        groups[i] = (n + GROUP - 1) // GROUP


def entry(lists, which, field, j):
    return lists[field * 2 * SLOTS + which * SLOTS + j]


def forward_kernel(which, lists, groups, blocks, g0, g1, g2, g3, out, nodes, acc):
    for i, part in enumerate((g0, g1, g2, g3)):
        nodes[4 * i : 4 * i + 4] = part[...]
    acc[...] = jnp.zeros_like(acc)

    def step(i, _):
        products = []
        for g in range(GROUP):
            j = i * GROUP + g
            product = dot(blocks[entry(lists, which, 0, j)], nodes[entry(lists, which, 2, j)])
            products.append((entry(lists, which, 1, j), product))
        for slot, product in products:
            acc[slot] += product
        return 0

    lax.fori_loop(0, groups[which], step, 0)
    out[...] = acc[0:16].astype(BF)


def middle_kernel(parts, weight, cotangent, output, spread):
    total = parts[0].astype(F32)
    for s in range(1, 16):
        total += parts[s].astype(F32)
    share = total.astype(BF)
    pre = dot(share, weight[...])
    sigma = 1.0 / (1.0 + jnp.exp(-pre))
    output[...] = (pre * sigma).astype(BF)
    slope = sigma * (1.0 + pre * (1.0 - sigma))
    slopes32 = cotangent[...].astype(F32) * slope
    slopes = slopes32.astype(BF)
    turned = slopes.astype(F32).T.astype(BF)
    grad = dot(share.astype(F32).T.astype(BF), slopes).astype(BF)
    for s in range(16):
        spread[s, 0:256, :] = turned
        spread[s, 256:272, :] = grad[16 * s : 16 * s + 16, 0:128]
        spread[s, 272:288, :] = grad[16 * s : 16 * s + 16, 128:256]


def split(value):
    high = value.astype(BF)
    return high, (value - high.astype(F32)).astype(BF)


def back_products(which, lists, groups, blocks, source, acc):
    def step(i, _):
        products = []
        for g in range(GROUP):
            j = i * GROUP + g
            product = dot(source[entry(lists, which, 3, j), 0:256, :], blocks[entry(lists, which, 0, j)])
            products.append((entry(lists, which, 4, j), product))
        for slot, product in products:
            acc[slot] += product
        return 0

    lax.fori_loop(0, groups[which], step, 0)


def backward_own_kernel(lists, groups, blocks, own, acc):
    acc[...] = jnp.zeros_like(acc)
    back_products(0, lists, groups, blocks, own, acc)


def backward_other_kernel(lists, groups, blocks, own, other, begun, b0, b1, b2, b3, acc):
    acc[...] = begun[...]
    back_products(1, lists, groups, blocks, other, acc)
    grad = jnp.zeros((32, 128), F32)
    for s in range(16):
        grad += own[s, 256:288, :].astype(F32) + other[s, 256:288, :].astype(F32)
    high, low = split(grad)
    for x, out in enumerate((b0, b1, b2, b3)):
        for z in range(4):
            out[256 * z : 256 * z + 256, :] = acc[4 * x + z].astype(BF)
        out[1024:1056, :] = high
        out[1056:1088, :] = low


def ordered_sum(me, parts, row, scratch):
    for k, part in enumerate(parts):
        high, low = part[row : row + 32, :], part[row + 32 : row + 64, :]
        scratch[(me - k) & 3] = high.astype(F32) + low.astype(F32)
    return scratch[0] + scratch[1] + scratch[2] + scratch[3]


def fold_kernel(info, b0, b1, b2, b3, f0, f1, f2, f3, scratch):
    parts = (b0, b1, b2, b3)
    high, low = split(ordered_sum(info[2], parts, 1024, scratch))
    for z, out in enumerate((f0, f1, f2, f3)):
        rows = slice(256 * z, 256 * z + 256)
        total = parts[0][rows, :].astype(F32)
        for part in parts[1:]:
            total += part[rows, :].astype(F32)
        out[0:256, :] = total.astype(BF)
        out[256:288, :] = high
        out[288:320, :] = low


def last_kernel(scale, info, f0, f1, f2, f3, weight, input_grad, grad_out, scratch):
    parts = (f0, f1, f2, f3)
    grad = ordered_sum(info[3], parts, 256, scratch) * scale
    for s in range(16):
        grad_out[s, :, 0:128] = grad[0:16]
        grad_out[s, :, 128:256] = grad[16:32]
    total = parts[0][0:256, :].astype(F32)
    for part in parts[1:]:
        total += part[0:256, :].astype(F32)
    back = total.astype(BF).astype(F32).T.astype(BF)
    input_grad[...] = dot(back, weight[...], (((1,), (1,)), ((), ()))).astype(BF)


def call(kernel, outs, kinds, scratch=(), flops=0, size=0):
    return pl.pallas_call(
        kernel,
        out_shape=[jax.ShapeDtypeStruct(s, d) for s, d, _ in outs],
        in_specs=kinds,
        out_specs=[k for _, _, k in outs],
        scratch_shapes=list(scratch),
        compiler_params=LIMIT,
        cost_estimate=pl.CostEstimate(flops=flops, bytes_accessed=size, transcendentals=0),
    )


def exchange(value, axes):
    return lax.all_to_all(value, axes, 0, 0, tiled=True)


def swap(value):
    return lax.ppermute(value, "c", [(0, 1), (1, 0)])


def rotate(value, axis, k):
    return lax.ppermute(value, axis, [(i, (i + k) % 4) for i in range(4)])


def shards(features, weight, cotangent, blocks, block_pos, counts):
    tile = blocks[0, 0]
    index = [lax.axis_index(a).astype(jnp.int32) for a in ("c", "x", "zl")]
    info = jnp.stack([counts[0, 0]] + index)
    nodes_total = 65536
    heavy = dict(flops=8 * 10**8, size=6 * 2**20)
    i32 = jnp.int32

    lists, groups = call(
        plan_kernel,
        [((10 * SLOTS,), i32, SMEM), ((2,), i32, SMEM)],
        [SMEM, SMEM],
        size=2**20,
    )(block_pos[0, 0], info)

    line = jnp.stack([features] + [rotate(features, "zl", k) for k in (1, 2, 3)])
    plane = [line] + [rotate(line, "x", k) for k in (1, 2, 3)]
    send, keep = [
        call(
            functools.partial(forward_kernel, which),
            [((16, 128, 256), BF, VMEM)],
            [SMEM, SMEM] + [VMEM] * 5,
            [pltpu.VMEM((16, 128, 256), BF), pltpu.VMEM((17, 128, 256), F32)],
            **heavy,
        )(lists, groups, tile, *plane)[0]
        for which in (1, 0)
    ]
    pair = (keep.astype(F32) + swap(send).astype(F32)).astype(BF)
    parts = exchange(pair, ("zh", "y"))
    output, spread = call(
        middle_kernel,
        [((128, 256), BF, VMEM), ((16, 288, 128), BF, VMEM)],
        [VMEM, VMEM, VMEM],
    )(parts, weight, cotangent)
    own = exchange(spread, ("zh", "y"))
    other = swap(own)
    (begun,) = call(
        backward_own_kernel,
        [((17, 256, 128), F32, VMEM)],
        [SMEM, SMEM, VMEM, VMEM],
        **heavy,
    )(lists, groups, tile, own)
    back = call(
        backward_other_kernel,
        [((1088, 128), BF, VMEM)] * 4,
        [SMEM, SMEM] + [VMEM] * 4,
        [pltpu.VMEM((17, 256, 128), F32)],
        **heavy,
    )(lists, groups, tile, own, other, begun)
    back = [back[0]] + [rotate(back[k], "x", k) for k in (1, 2, 3)]
    folded = call(
        fold_kernel,
        [((320, 128), BF, VMEM)] * 4,
        [SMEM] + [VMEM] * 4,
        [pltpu.VMEM((4, 32, 128), F32)],
    )(info, *back)
    folded = [folded[0]] + [rotate(folded[k], "zl", k) for k in (1, 2, 3)]
    input_grad, grad = call(
        functools.partial(last_kernel, 1.0 / math.sqrt(nodes_total)),
        [((128, 256), BF, VMEM), ((16, 16, 256), F32, VMEM)],
        [SMEM] + [VMEM] * 5,
        [pltpu.VMEM((4, 32, 128), F32)],
    )(info, *folded, weight)
    weight_grad = exchange(grad, ("zh", "y")).reshape(256, 256)
    return (output, input_grad, weight_grad)


def solution(mesh):
    names = ("zl", "x", "zh", "y", "c")
    row, col = names[:2], names[2:]
    fine = Mesh(mesh.devices.reshape(4, 4, 2, 8, 2), names)
    return jax.shard_map(
        shards,
        mesh=fine,
        in_specs=(
            P(col + row, None),
            P(),
            P(row + col, None),
            P(row, col, None, None, None),
            P(row, col, None),
            P(row, col),
        ),
        out_specs=(P(row + col, None), P(col + row, None), P()),
        check_vma=False,
    )
```

```python
import functools
import math

import jax
import jax.numpy as jnp
from jax import lax
from jax.experimental import pallas as pl
from jax.experimental.pallas import tpu as pltpu
from jax.sharding import Mesh
from jax.sharding import PartitionSpec as P

BF = jnp.bfloat16
F32 = jnp.float32
GROUP = 16
SLOTS = 112
VMEM = pl.BlockSpec(memory_space=pltpu.VMEM)
SMEM = pl.BlockSpec(memory_space=pltpu.SMEM)
LIMIT = pltpu.CompilerParams(vmem_limit_bytes=20 * 1024 * 1024)


def dot(a, b, dims=(((1,), (0,)), ((), ()))):
    return lax.dot_general(a, b, dims, preferred_element_type=F32)


def plan_kernel(place, info, blocks, lists, groups):
    count, core, xi, zi = info[0], info[1], info[2], info[3]

    def write(at, k, t, source, half, target):
        for f, value in enumerate((k, t, source, half, target)):
            lists[f * 2 * SLOTS + at] = value

    def step(k, held):
        p = place[k]
        t, a = p >> 4, p & 15
        z, x = a >> 2, a & 3
        half = t >> 1
        source = (((xi - x) & 3) << 2) + ((zi - z) & 3)
        target = (((x - xi) & 3) << 2) + ((z - zi) & 3)
        mine, theirs = held
        away = (t & 1) ^ core
        write(jnp.where(away == 0, mine, SLOTS + theirs), k, half, source, half, target)
        return mine + 1 - away, theirs + away

    mine, theirs = lax.fori_loop(0, count, step, (jnp.int32(0), jnp.int32(0)))
    for i, n in enumerate((mine, theirs)):
        for g in range(GROUP):
            write(i * SLOTS + n + g, 0, 16, 0, 0, 16)
        groups[i] = (n + GROUP - 1) // GROUP


def entry(lists, which, field, j):
    return lists[field * 2 * SLOTS + which * SLOTS + j]


def products_into(acc, lists, groups, which, target, product):
    def step(i, _):
        products = []
        for g in range(GROUP):
            j = i * GROUP + g
            products.append((entry(lists, which, target, j), product(j)))
        for slot, value in products:
            acc[slot] += value
        return 0

    lax.fori_loop(0, groups[which], step, 0)


def line_kernel(f0, f1, f2, f3, line0, line1):
    for k, part in enumerate((f0, f1, f2, f3)):
        line0[k] = part[:, 0:128]
        line1[k] = part[:, 128:256]


def forward_products(which, lists, groups, blocks, parts, out, nodes, acc):
    for i, part in enumerate(parts):
        nodes[4 * i : 4 * i + 4] = part[...]
    acc[...] = jnp.zeros_like(acc)

    def product(j):
        return dot(blocks[entry(lists, which, 0, j)], nodes[entry(lists, which, 2, j)])

    products_into(acc, lists, groups, which, 1, product)
    out[...] = acc[0:16].astype(BF)


def forward_kernel(which, lists, groups, blocks, g0, g1, g2, g3, out, nodes, acc):
    forward_products(which, lists, groups, blocks, (g0, g1, g2, g3), out, nodes, acc)


def forward_gate_kernel(which, lists, groups, blocks, g0, g1, g2, g3, later, out, now, nodes, acc):
    now[...] = later[...]
    forward_products(which, lists, groups, blocks, (g0, g1, g2, g3), out, nodes, acc)


def middle_kernel(parts0, parts1, weight, cotangent, output, spread0, spread1):
    shares = []
    for parts in (parts0, parts1):
        total = parts[0].astype(F32)
        for s in range(1, 16):
            total += parts[s].astype(F32)
        shares.append(total.astype(BF))
    share = jnp.concatenate(shares, axis=1)
    pre = dot(share, weight[...])
    sigma = 1.0 / (1.0 + jnp.exp(-pre))
    output[...] = (pre * sigma).astype(BF)
    slope = sigma * (1.0 + pre * (1.0 - sigma))
    slopes = (cotangent[...].astype(F32) * slope).astype(BF)
    turned = slopes.astype(F32).T.astype(BF)
    grad = dot(share.astype(F32).T.astype(BF), slopes).astype(BF)
    for s in range(16):
        spread0[s, 0:128, :] = turned[0:128]
        spread0[s, 128:144, :] = grad[16 * s : 16 * s + 16, 0:128]
        spread0[s, 144:160, :] = grad[16 * s : 16 * s + 16, 128:256]
        spread1[s] = turned[128:256]


def split(value):
    high = value.astype(BF)
    return high, (value - high.astype(F32)).astype(BF)


def back_products(which, lists, groups, blocks, source, acc):
    def product(j):
        return dot(source[entry(lists, which, 3, j), 0:128, :], blocks[entry(lists, which, 0, j)])

    products_into(acc, lists, groups, which, 4, product)


def backward_own_kernel(lists, groups, blocks, own, acc):
    acc[...] = jnp.zeros_like(acc)
    back_products(0, lists, groups, blocks, own, acc)


def backward_other_kernel(lists, groups, blocks, own, other, begun, b0, b1, b2, b3, acc):
    acc[...] = begun[...]
    back_products(1, lists, groups, blocks, other, acc)
    for x, out in enumerate((b0, b1, b2, b3)):
        for z in range(4):
            out[128 * z : 128 * z + 128, :] = acc[4 * x + z].astype(BF)
    if own.shape[1] > 128:
        grad = jnp.zeros((32, 128), F32)
        for s in range(16):
            grad += own[s, 128:160, :].astype(F32) + other[s, 128:160, :].astype(F32)
        high, low = split(grad)
        for out in (b0, b1, b2, b3):
            out[512:544, :] = high
            out[544:576, :] = low


def ordered_sum(me, parts, row, scratch):
    for k, part in enumerate(parts):
        high, low = part[row : row + 32, :], part[row + 32 : row + 64, :]
        scratch[(me - k) & 3] = high.astype(F32) + low.astype(F32)
    return scratch[0] + scratch[1] + scratch[2] + scratch[3]


def fold_kernel(info, b0, b1, b2, b3, f0, f1, f2, f3, scratch):
    parts, outs = (b0, b1, b2, b3), (f0, f1, f2, f3)
    for z, out in enumerate(outs):
        rows = slice(128 * z, 128 * z + 128)
        total = parts[0][rows, :].astype(F32)
        for part in parts[1:]:
            total += part[rows, :].astype(F32)
        out[0:128, :] = total.astype(BF)
    if b0.shape[0] > 512:
        high, low = split(ordered_sum(info[2], parts, 512, scratch))
        for out in outs:
            out[128:160, :] = high
            out[160:192, :] = low


def fold_gate_kernel(info, b0, b1, b2, b3, later, f0, f1, f2, f3, now, scratch):
    now[...] = later[...]
    fold_kernel(info, b0, b1, b2, b3, f0, f1, f2, f3, scratch)


def grad_kernel(scale, info, f0, f1, f2, f3, grad_out, scratch):
    grad = ordered_sum(info[3], (f0, f1, f2, f3), 128, scratch) * scale
    for s in range(16):
        grad_out[s, :, 0:128] = grad[0:16]
        grad_out[s, :, 128:256] = grad[16:32]


def last_kernel(f0, f1, f2, f3, h0, h1, h2, h3, weight, input_grad):
    backs = []
    for parts in ((f0, f1, f2, f3), (h0, h1, h2, h3)):
        total = parts[0][0:128, :].astype(F32)
        for part in parts[1:]:
            total += part[0:128, :].astype(F32)
        backs.append(total.astype(BF).astype(F32).T.astype(BF))
    back = jnp.concatenate(backs, axis=1)
    input_grad[...] = dot(back, weight[...], (((1,), (1,)), ((), ()))).astype(BF)


def call(kernel, outs, kinds, scratch=(), flops=0, size=0):
    return pl.pallas_call(
        kernel,
        out_shape=[jax.ShapeDtypeStruct(s, d) for s, d, _ in outs],
        in_specs=kinds,
        out_specs=[k for _, _, k in outs],
        scratch_shapes=list(scratch),
        compiler_params=LIMIT,
        cost_estimate=pl.CostEstimate(flops=flops, bytes_accessed=size, transcendentals=0),
    )


def exchange(value, axes):
    return lax.all_to_all(value, axes, 0, 0, tiled=True)


def swap(value):
    return lax.ppermute(value, "c", [(0, 1), (1, 0)])


def rotate(value, axis, k):
    return lax.ppermute(value, axis, [(i, (i + k) % 4) for i in range(4)])


def shards(features, weight, cotangent, blocks, block_pos, counts):
    tile = blocks[0, 0]
    index = [lax.axis_index(a).astype(jnp.int32) for a in ("c", "x", "zl")]
    info = jnp.stack([counts[0, 0]] + index)
    nodes_total = 65536
    heavy = dict(flops=4 * 10**8, size=4 * 2**20)
    i32 = jnp.int32
    rounds = (1, 2, 3)

    lists, groups = call(
        plan_kernel,
        [((10 * SLOTS,), i32, SMEM), ((2,), i32, SMEM)],
        [SMEM, SMEM, VMEM],
        size=2**20,
    )(block_pos[0, 0], info, tile)

    line = [features] + [rotate(features, "zl", k) for k in rounds]
    line0, line1 = call(line_kernel, [((4, 128, 128), BF, VMEM)] * 2, [VMEM] * 4)(*line)
    kept = ((16, 128, 128), BF, VMEM)
    scratch = [pltpu.VMEM((16, 128, 128), BF), pltpu.VMEM((17, 128, 128), F32)]
    kinds = [SMEM, SMEM] + [VMEM] * 5

    def forward(which, plane):
        body = functools.partial(forward_kernel, which)
        return call(body, [kept], kinds, scratch, **heavy)(lists, groups, tile, *plane)[0]

    plane = [line0] + [rotate(line0, "x", k) for k in rounds]
    send, line1 = call(
        functools.partial(forward_gate_kernel, 1),
        [kept, ((4, 128, 128), BF, VMEM)],
        kinds + [VMEM],
        scratch,
        **heavy,
    )(lists, groups, tile, *plane, line1)
    plane1 = [line1] + [rotate(line1, "x", k) for k in rounds]
    sent = swap(send)
    pair = (forward(0, plane).astype(F32) + sent.astype(F32)).astype(BF)
    parts0 = exchange(pair, ("zh", "y"))
    sent = swap(forward(1, plane1))
    pair = (forward(0, plane1).astype(F32) + sent.astype(F32)).astype(BF)
    parts1 = exchange(pair, ("zh", "y"))
    output, spread0, spread1 = call(
        middle_kernel,
        [((128, 256), BF, VMEM), ((16, 160, 128), BF, VMEM), ((16, 128, 128), BF, VMEM)],
        [VMEM] * 4,
    )(parts0, parts1, weight, cotangent)

    def backward(own):
        other = swap(own)
        (begun,) = call(
            backward_own_kernel,
            [((17, 128, 128), F32, VMEM)],
            [SMEM, SMEM, VMEM, VMEM],
            **heavy,
        )(lists, groups, tile, own)
        rows = 512 + (64 if own.shape[1] > 128 else 0)
        back = call(
            backward_other_kernel,
            [((rows, 128), BF, VMEM)] * 4,
            [SMEM, SMEM] + [VMEM] * 4,
            [pltpu.VMEM((17, 128, 128), F32)],
            **heavy,
        )(lists, groups, tile, own, other, begun)
        return [back[0]] + [rotate(back[k], "x", k) for k in rounds]

    small = [pltpu.VMEM((4, 32, 128), F32)]
    own0 = exchange(spread0, ("zh", "y"))
    own1 = exchange(spread1, ("zh", "y"))
    *fold0, own1 = call(
        fold_gate_kernel,
        [((192, 128), BF, VMEM)] * 4 + [((16, 128, 128), BF, VMEM)],
        [SMEM] + [VMEM] * 5,
        small,
    )(info, *backward(own0), own1)
    fold0[1:] = [rotate(fold0[k], "zl", k) for k in rounds]
    fold1 = call(fold_kernel, [((128, 128), BF, VMEM)] * 4, [SMEM] + [VMEM] * 4, small)(info, *backward(own1))
    fold1 = [fold1[0]] + [rotate(fold1[k], "zl", k) for k in rounds]
    folds = (fold0, fold1)
    (grad,) = call(
        functools.partial(grad_kernel, 1.0 / math.sqrt(nodes_total)),
        [((16, 16, 256), F32, VMEM)],
        [SMEM] + [VMEM] * 4,
        [pltpu.VMEM((4, 32, 128), F32)],
    )(info, *folds[0])
    weight_grad = exchange(grad, ("zh", "y")).reshape(256, 256)
    (input_grad,) = call(
        last_kernel,
        [((128, 256), BF, VMEM)],
        [VMEM] * 9,
    )(*folds[0], *folds[1], weight)
    return (output, input_grad, weight_grad)


def solution(mesh):
    names = ("zl", "x", "zh", "y", "c")
    row, col = names[:2], names[2:]
    fine = Mesh(mesh.devices.reshape(4, 4, 2, 8, 2), names)
    return jax.shard_map(
        shards,
        mesh=fine,
        in_specs=(
            P(col + row, None),
            P(),
            P(row + col, None),
            P(row, col, None, None, None),
            P(row, col, None),
            P(row, col),
        ),
        out_specs=(P(row + col, None), P(col + row, None), P()),
        check_vma=False,
    )
```

```python
import functools
import math

import jax
import jax.numpy as jnp
from jax import lax
from jax.experimental import pallas as pl
from jax.experimental.pallas import tpu as pltpu
from jax.sharding import Mesh
from jax.sharding import PartitionSpec as P

BF = jnp.bfloat16
F32 = jnp.float32
GROUP = 16
SLOTS = 112
VMEM = pl.BlockSpec(memory_space=pltpu.VMEM)
SMEM = pl.BlockSpec(memory_space=pltpu.SMEM)
LIMIT = pltpu.CompilerParams(vmem_limit_bytes=48 * 1024 * 1024)


def dot(a, b, dims=(((1,), (0,)), ((), ()))):
    return lax.dot_general(a, b, dims, preferred_element_type=F32)


def plan_kernel(place, info, blocks, lists, groups):
    count, core, xi, zi = info[0], info[1], info[2], info[3]

    def write(at, k, t, source, half, target):
        for f, value in enumerate((k, t, source, half, target)):
            lists[f * 2 * SLOTS + at] = value

    def step(k, held):
        p = place[k]
        t, a = p >> 4, p & 15
        z, x = a >> 2, a & 3
        half = t >> 1
        source = (x << 2) + z
        target = (((x - xi) & 3) << 2) + ((z - zi) & 3)
        mine, theirs = held
        away = (t & 1) ^ core
        write(jnp.where(away == 0, mine, SLOTS + theirs), k, half, source, half, target)
        return mine + 1 - away, theirs + away

    mine, theirs = lax.fori_loop(0, count, step, (jnp.int32(0), jnp.int32(0)))
    for i, n in enumerate((mine, theirs)):
        for g in range(GROUP):
            write(i * SLOTS + n + g, 0, 16, 0, 0, 16)
        groups[i] = (n + GROUP - 1) // GROUP


def entry(lists, which, field, j):
    return lists[field * 2 * SLOTS + which * SLOTS + j]


def forward_kernel(which, lists, groups, blocks, nodes, out, acc):
    acc[...] = jnp.zeros_like(acc)

    def step(i, _):
        products = []
        for g in range(GROUP):
            j = i * GROUP + g
            product = dot(blocks[entry(lists, which, 0, j)], nodes[entry(lists, which, 2, j)])
            products.append((entry(lists, which, 1, j), product))
        for slot, product in products:
            acc[slot] += product
        return 0

    lax.fori_loop(0, groups[which], step, 0)
    out[...] = acc[0:16].astype(BF)


def middle_kernel(parts, weight, cotangent, output, spread):
    total = parts[0].astype(F32)
    for s in range(1, 16):
        total += parts[s].astype(F32)
    share = total.astype(BF)
    pre = dot(share, weight[...])
    sigma = 1.0 / (1.0 + jnp.exp(-pre))
    output[...] = (pre * sigma).astype(BF)
    slope = sigma * (1.0 + pre * (1.0 - sigma))
    slopes32 = cotangent[...].astype(F32) * slope
    slopes = slopes32.astype(BF)
    turned = slopes.astype(F32).T.astype(BF)
    grad = dot(share.astype(F32).T.astype(BF), slopes).astype(BF)
    for s in range(16):
        spread[s, 0:256, :] = turned
        rows = slice(32 * (s % 8), 32 * (s % 8) + 32)
        spread[s, 256:288, :] = grad[rows, 0:128]
        spread[s, 288:320, :] = grad[rows, 128:256]


def split(value):
    high = value.astype(BF)
    return high, (value - high.astype(F32)).astype(BF)


def back_products(which, lists, groups, blocks, source, acc):
    def step(i, _):
        products = []
        for g in range(GROUP):
            j = i * GROUP + g
            product = dot(source[entry(lists, which, 3, j), 0:256, :], blocks[entry(lists, which, 0, j)])
            products.append((entry(lists, which, 4, j), product))
        for slot, product in products:
            acc[slot] += product
        return 0

    lax.fori_loop(0, groups[which], step, 0)


def backward_own_kernel(lists, groups, blocks, own, acc):
    acc[...] = jnp.zeros_like(acc)
    back_products(0, lists, groups, blocks, own, acc)


def backward_other_kernel(lists, groups, blocks, own, other, begun, b0, b1, b2, b3, acc):
    back_products(1, lists, groups, blocks, other, acc)
    grad = jnp.zeros((64, 128), F32)
    for s in range(16):
        grad += own[s, 256:320, :].astype(F32) + other[s, 256:320, :].astype(F32)
    high, low = split(grad)
    for x, out in enumerate((b0, b1, b2, b3)):
        for z in range(4):
            out[256 * z : 256 * z + 256, :] = acc[4 * x + z].astype(BF)
        out[1024:1088, :] = high
        out[1088:1152, :] = low


def ordered_sum(me, parts, row, scratch):
    for k, part in enumerate(parts):
        high, low = part[row : row + 64, :], part[row + 64 : row + 128, :]
        scratch[(me - k) & 3] = high.astype(F32) + low.astype(F32)
    return scratch[0] + scratch[1] + scratch[2] + scratch[3]


def fold_kernel(info, b0, b1, b2, b3, f0, f1, f2, f3, scratch):
    parts = (b0, b1, b2, b3)
    high, low = split(ordered_sum(info[2], parts, 1024, scratch))
    for z, out in enumerate((f0, f1, f2, f3)):
        rows = slice(256 * z, 256 * z + 256)
        total = parts[0][rows, :].astype(F32)
        for part in parts[1:]:
            total += part[rows, :].astype(F32)
        out[0:256, :] = total.astype(BF)
        out[256:320, :] = high
        out[320:384, :] = low


def grad_kernel(scale, info, f0, f1, f2, f3, grad_out, scratch):
    grad = (ordered_sum(info[3], (f0, f1, f2, f3), 256, scratch) * scale).astype(BF)
    for s in range(8):
        grad_out[s, :, 0:128] = grad[0:32]
        grad_out[s, :, 128:256] = grad[32:64]


def last_kernel(f0, f1, f2, f3, weight, input_grad):
    total = f0[0:256, :].astype(F32)
    for part in (f1, f2, f3):
        total += part[0:256, :].astype(F32)
    back = total.astype(BF).astype(F32).T.astype(BF)
    input_grad[...] = dot(back, weight[...], (((1,), (1,)), ((), ()))).astype(BF)


def call(kernel, outs, kinds, scratch=(), flops=0, size=0, alias=None):
    return pl.pallas_call(
        kernel,
        out_shape=[jax.ShapeDtypeStruct(s, d) for s, d, _ in outs],
        in_specs=kinds,
        out_specs=[k for _, _, k in outs],
        scratch_shapes=list(scratch),
        input_output_aliases=alias or {},
        compiler_params=LIMIT,
        cost_estimate=pl.CostEstimate(flops=flops, bytes_accessed=size, transcendentals=0),
    )


def exchange(value, axes):
    return lax.all_to_all(value, axes, 0, 0, tiled=True)


def swap(value):
    return lax.ppermute(value, "c", [(0, 1), (1, 0)])


def rotate(value, axis, k):
    return lax.ppermute(value, axis, [(i, (i + k) % 4) for i in range(4)])


def shards(features, weight, cotangent, blocks, block_pos, counts):
    tile = blocks[0, 0]
    index = [lax.axis_index(a).astype(jnp.int32) for a in ("c", "x", "zl")]
    info = jnp.stack([counts[0, 0]] + index)
    nodes_total = 65536
    heavy = dict(flops=8 * 10**8, size=6 * 2**20)
    i32 = jnp.int32

    lists, groups = call(
        plan_kernel,
        [((10 * SLOTS,), i32, SMEM), ((2,), i32, SMEM)],
        [SMEM, SMEM, VMEM],
        size=2**20,
    )(block_pos[0, 0], info, tile)

    line = exchange(jnp.broadcast_to(features[None], (4, 128, 256)), "zl")
    nodes = exchange(jnp.broadcast_to(line[None], (4, 4, 128, 256)), "x").reshape(16, 128, 256)
    send, keep = [
        call(
            functools.partial(forward_kernel, which),
            [((16, 128, 256), BF, VMEM)],
            [SMEM, SMEM, VMEM, VMEM],
            [pltpu.VMEM((17, 128, 256), F32)],
            **heavy,
        )(lists, groups, tile, nodes)[0]
        for which in (1, 0)
    ]
    pair = (keep.astype(F32) + swap(send).astype(F32)).astype(BF)
    parts = exchange(pair, ("zh", "y"))
    output, spread = call(
        middle_kernel,
        [((128, 256), BF, VMEM), ((16, 320, 128), BF, VMEM)],
        [VMEM, VMEM, VMEM],
    )(parts, weight, cotangent)
    own = exchange(spread, ("zh", "y"))
    other = swap(own)
    (begun,) = call(
        backward_own_kernel,
        [((17, 256, 128), F32, VMEM)],
        [SMEM, SMEM, VMEM, VMEM],
        **heavy,
    )(lists, groups, tile, own)
    back = call(
        backward_other_kernel,
        [((1152, 128), BF, VMEM)] * 4 + [((17, 256, 128), F32, VMEM)],
        [SMEM, SMEM] + [VMEM] * 4,
        alias={5: 4},
        **heavy,
    )(lists, groups, tile, own, other, begun)
    back = [back[0]] + [rotate(back[k], "x", k) for k in (1, 2, 3)]
    folded = call(
        fold_kernel,
        [((384, 128), BF, VMEM)] * 4,
        [SMEM] + [VMEM] * 4,
        [pltpu.VMEM((4, 64, 128), F32)],
    )(info, *back)
    folded = [folded[0]] + [rotate(folded[k], "zl", k) for k in (1, 2, 3)]
    (grad,) = call(
        functools.partial(grad_kernel, 1.0 / math.sqrt(nodes_total)),
        [((8, 32, 256), BF, VMEM)],
        [SMEM] + [VMEM] * 4,
        [pltpu.VMEM((4, 64, 128), F32)],
    )(info, *folded)
    weight_grad = exchange(grad, "y").reshape(256, 256).astype(F32)
    (input_grad,) = call(last_kernel, [((128, 256), BF, VMEM)], [VMEM] * 5, flops=2**24, size=2**20)(*folded, weight)
    return (output, input_grad, weight_grad)


def solution(mesh):
    names = ("zl", "x", "zh", "y", "c")
    row, col = names[:2], names[2:]
    fine = Mesh(mesh.devices.reshape(4, 4, 2, 8, 2), names)
    return jax.shard_map(
        shards,
        mesh=fine,
        in_specs=(
            P(col + row, None),
            P(),
            P(row + col, None),
            P(row, col, None, None, None),
            P(row, col, None),
            P(row, col),
        ),
        out_specs=(P(row + col, None), P(col + row, None), P()),
        check_vma=False,
    )
```

```python
import functools
import math

import jax
import jax.numpy as jnp
from jax import lax
from jax.experimental import pallas as pl
from jax.experimental.pallas import tpu as pltpu
from jax.sharding import Mesh
from jax.sharding import PartitionSpec as P

BF = jnp.bfloat16
F32 = jnp.float32
GROUP = 16
SLOTS = 112
VMEM = pl.BlockSpec(memory_space=pltpu.VMEM)
SMEM = pl.BlockSpec(memory_space=pltpu.SMEM)
LIMIT = pltpu.CompilerParams(vmem_limit_bytes=48 * 1024 * 1024)


def dot(a, b, dims=(((1,), (0,)), ((), ()))):
    return lax.dot_general(a, b, dims, preferred_element_type=F32)


def plan_kernel(place, info, blocks, lists, groups):
    count, core, xi, zi, odd = info[0], info[1], info[2], info[3], info[4]

    def write(at, k, t, source, half, target):
        for f, value in enumerate((k, t, source, half, target)):
            lists[f * 2 * SLOTS + at] = value

    def step(k, held):
        p = place[k]
        t, a = p >> 4, p & 15
        z, x = a >> 2, a & 3
        half = (((t >> 1 & 1) ^ odd) << 3) + (t >> 2)
        source = (x << 2) + z
        target = (((x - xi) & 3) << 2) + ((z - zi) & 3)
        mine, theirs = held
        away = (t & 1) ^ core
        write(jnp.where(away == 0, mine, SLOTS + theirs), k, half, source, half, target)
        return mine + 1 - away, theirs + away

    mine, theirs = lax.fori_loop(0, count, step, (jnp.int32(0), jnp.int32(0)))
    for i, n in enumerate((mine, theirs)):
        for g in range(GROUP):
            write(i * SLOTS + n + g, 0, 16, 0, 0, 16)
        groups[i] = (n + GROUP - 1) // GROUP


def entry(lists, which, field, j):
    return lists[field * 2 * SLOTS + which * SLOTS + j]


def forward_kernel(which, lists, groups, blocks, nodes, out, acc):
    acc[...] = jnp.zeros_like(acc)

    def step(i, _):
        products = []
        for g in range(GROUP):
            j = i * GROUP + g
            product = dot(blocks[entry(lists, which, 0, j)], nodes[entry(lists, which, 2, j)])
            products.append((entry(lists, which, 1, j), product))
        for slot, product in products:
            acc[slot] += product
        return 0

    lax.fori_loop(0, groups[which], step, 0)
    out[...] = acc[0:16].astype(BF)


def middle_kernel(parts, weight, cotangent, output, spread):
    total = parts[0].astype(F32)
    for s in range(1, 8):
        total += parts[s].astype(F32)
    share = total.astype(BF)
    pre = dot(share, weight[...])
    sigma = 1.0 / (1.0 + jnp.exp(-pre))
    output[...] = (pre * sigma).astype(BF)
    slope = sigma * (1.0 + pre * (1.0 - sigma))
    slopes32 = cotangent[...].astype(F32) * slope
    slopes = slopes32.astype(BF)
    turned = slopes.astype(F32).T.astype(BF)
    columns = share.astype(F32).T.astype(BF)
    for s in range(8):
        spread[s, 0:128, :] = turned[0:128]
        spread[s, 128:192, :] = columns[64 * (s % 4) : 64 * (s % 4) + 64]
        spread[s, 192:320, :] = turned[128:256]


def back_products(which, lists, groups, blocks, same, near, far, source, acc):
    source[0:8, 0:128, :] = same[:, 0:128, :]
    source[0:8, 128:256, :] = same[:, 192:320, :]
    source[8:16, 0:128, :] = near[:, 0:128, :]
    source[8:16, 128:256, :] = far[...]

    def step(i, _):
        products = []
        for g in range(GROUP):
            j = i * GROUP + g
            product = dot(source[entry(lists, which, 3, j)], blocks[entry(lists, which, 0, j)])
            products.append((entry(lists, which, 4, j), product))
        for slot, product in products:
            acc[slot] += product
        return 0

    lax.fori_loop(0, groups[which], step, 0)
    sums = []
    for first, part in ((0, same), (8, near)):
        total = jnp.zeros((64, 256), F32)
        for s in range(8):
            total += dot(part[s, 128:192, :], source[first + s], (((1,), (1,)), ((), ())))
        sums.append(total)
    return sums[0] + sums[1]


def backward_own_kernel(lists, groups, blocks, same, near, far, acc, grad, source):
    acc[...] = jnp.zeros_like(acc)
    grad[...] = back_products(0, lists, groups, blocks, same, near, far, source, acc)


def backward_other_kernel(lists, groups, blocks, same, near, far, half, begun, b0, b1, b2, b3, acc, source):
    grad = back_products(1, lists, groups, blocks, same, near, far, source, acc)
    grad = (half[...] + grad).astype(BF)
    for x, out in enumerate((b0, b1, b2, b3)):
        for z in range(4):
            out[256 * z : 256 * z + 256, :] = acc[4 * x + z].astype(BF)
        out[1024:1088, :] = grad[:, 0:128]
        out[1088:1152, :] = grad[:, 128:256]


def ordered_sum(me, parts, row, scratch):
    for k, part in enumerate(parts):
        scratch[(me - k) & 3] = part[row : row + 128, :].astype(F32)
    return scratch[0] + scratch[1] + scratch[2] + scratch[3]


def fold_kernel(info, b0, b1, b2, b3, f0, f1, f2, f3, scratch):
    parts = (b0, b1, b2, b3)
    grad = ordered_sum(info[2], parts, 1024, scratch).astype(BF)
    for z, out in enumerate((f0, f1, f2, f3)):
        rows = slice(256 * z, 256 * z + 256)
        total = parts[0][rows, :].astype(F32)
        for part in parts[1:]:
            total += part[rows, :].astype(F32)
        out[0:256, :] = total.astype(BF)
        out[256:384, :] = grad


def grad_kernel(scale, info, f0, f1, f2, f3, grad_out, scratch):
    grad = (ordered_sum(info[3], (f0, f1, f2, f3), 256, scratch) * scale).astype(BF)
    for s in range(4):
        grad_out[s, :, 0:128] = grad[0:64]
        grad_out[s, :, 128:256] = grad[64:128]


def last_kernel(f0, f1, f2, f3, weight, input_grad):
    total = f0[0:256, :].astype(F32)
    for part in (f1, f2, f3):
        total += part[0:256, :].astype(F32)
    back = total.astype(BF).astype(F32).T.astype(BF)
    input_grad[...] = dot(back, weight[...], (((1,), (1,)), ((), ()))).astype(BF)


def call(kernel, outs, kinds, scratch=(), flops=0, size=0, alias=None):
    return pl.pallas_call(
        kernel,
        out_shape=[jax.ShapeDtypeStruct(s, d) for s, d, _ in outs],
        in_specs=kinds,
        out_specs=[k for _, _, k in outs],
        scratch_shapes=list(scratch),
        input_output_aliases=alias or {},
        compiler_params=LIMIT,
        cost_estimate=pl.CostEstimate(flops=flops, bytes_accessed=size, transcendentals=0),
    )


def exchange(value, axes):
    return lax.all_to_all(value, axes, 0, 0, tiled=True)


def swap(value):
    return lax.ppermute(value, "c", [(0, 1), (1, 0)])


def near(value):
    return lax.ppermute(value, "yl", [(0, 1), (1, 0)])


def far(value):
    return lax.ppermute(value, ("yh", "yl"), [(y, (y + 2 * (y % 2) - 1) % 8) for y in range(8)])


def rotate(value, axis, k):
    return lax.ppermute(value, axis, [(i, (i + k) % 4) for i in range(4)])


def shards(features, weight, cotangent, blocks, block_pos, counts):
    tile = blocks[0, 0]
    index = [lax.axis_index(a).astype(jnp.int32) for a in ("c", "x", "zl", "yl")]
    info = jnp.stack([counts[0, 0]] + index)
    nodes_total = 65536
    heavy = dict(flops=8 * 10**8, size=6 * 2**20)
    i32 = jnp.int32

    lists, groups = call(
        plan_kernel,
        [((10 * SLOTS,), i32, SMEM), ((2,), i32, SMEM)],
        [SMEM, SMEM, VMEM],
        size=2**20,
    )(block_pos[0, 0], info, tile)

    line = exchange(jnp.broadcast_to(features[None], (4, 128, 256)), "zl")
    nodes = exchange(jnp.broadcast_to(line[None], (4, 4, 128, 256)), "x").reshape(16, 128, 256)
    send, keep = [
        call(
            functools.partial(forward_kernel, which),
            [((16, 128, 256), BF, VMEM)],
            [SMEM, SMEM, VMEM, VMEM],
            [pltpu.VMEM((17, 128, 256), F32)],
            **heavy,
        )(lists, groups, tile, nodes)[0]
        for which in (1, 0)
    ]
    pair = keep.astype(F32) + swap(send).astype(F32)
    go = pair[8:].astype(BF)
    came = jnp.concatenate([near(go[:, :, :128]), far(go[:, :, 128:])], axis=2)
    parts = exchange((pair[:8] + came.astype(F32)).astype(BF), ("zh", "yh"))
    output, spread = call(
        middle_kernel,
        [((128, 256), BF, VMEM), ((8, 320, 128), BF, VMEM)],
        [VMEM, VMEM, VMEM],
    )(parts, weight, cotangent)
    same = exchange(spread, ("zh", "yh"))
    own = [same, near(same[:, :192]), far(same[:, 192:])]
    other = [swap(part) for part in own]
    source = pltpu.VMEM((16, 256, 128), BF)
    begun, half = call(
        backward_own_kernel,
        [((17, 256, 128), F32, VMEM), ((64, 256), F32, VMEM)],
        [SMEM, SMEM] + [VMEM] * 4,
        [source],
        **heavy,
    )(lists, groups, tile, *own)
    back = call(
        backward_other_kernel,
        [((1152, 128), BF, VMEM)] * 4 + [((17, 256, 128), F32, VMEM)],
        [SMEM, SMEM] + [VMEM] * 6,
        [source],
        alias={7: 4},
        **heavy,
    )(lists, groups, tile, *other, half, begun)
    back = [back[0]] + [rotate(back[k], "x", k) for k in (1, 2, 3)]
    folded = call(
        fold_kernel,
        [((384, 128), BF, VMEM)] * 4,
        [SMEM] + [VMEM] * 4,
        [pltpu.VMEM((4, 128, 128), F32)],
    )(info, *back)
    folded = [folded[0]] + [rotate(folded[k], "zl", k) for k in (1, 2, 3)]
    (grad,) = call(
        functools.partial(grad_kernel, 1.0 / math.sqrt(nodes_total)),
        [((4, 64, 256), BF, VMEM)],
        [SMEM] + [VMEM] * 4,
        [pltpu.VMEM((4, 128, 128), F32)],
    )(info, *folded)
    weight_grad = exchange(grad, "yh").reshape(256, 256).astype(F32)
    (input_grad,) = call(last_kernel, [((128, 256), BF, VMEM)], [VMEM] * 5, flops=2**24, size=2**20)(*folded, weight)
    return (output, input_grad, weight_grad)


def solution(mesh):
    names = ("zl", "x", "zh", "yh", "yl", "c")
    row, col = names[:2], names[2:]
    fine = Mesh(mesh.devices.reshape(4, 4, 2, 4, 2, 2), names)
    return jax.shard_map(
        shards,
        mesh=fine,
        in_specs=(
            P(col + row, None),
            P(),
            P(row + col, None),
            P(row, col, None, None, None),
            P(row, col, None),
            P(row, col),
        ),
        out_specs=(P(row + col, None), P(col + row, None), P()),
        check_vma=False,
    )
```

```python
import functools
import math

import jax
import jax.numpy as jnp
from jax import lax
from jax.experimental import pallas as pl
from jax.experimental.pallas import tpu as pltpu
from jax.sharding import Mesh
from jax.sharding import PartitionSpec as P

BF = jnp.bfloat16
F32 = jnp.float32
GROUP = 16
SLOTS = 112
VMEM = pl.BlockSpec(memory_space=pltpu.VMEM)
SMEM = pl.BlockSpec(memory_space=pltpu.SMEM)
LIMIT = pltpu.CompilerParams(vmem_limit_bytes=48 * 1024 * 1024)


def dot(a, b, dims=(((1,), (0,)), ((), ()))):
    return lax.dot_general(a, b, dims, preferred_element_type=F32)


def plan_kernel(place, info, blocks, lists, groups):
    count, core = info[0], info[1]

    def write(at, k, t, source, half, target):
        for f, value in enumerate((k, t, source, half, target)):
            lists[f * 2 * SLOTS + at] = value

    def step(k, held):
        p = place[k]
        t, a = p >> 4, p & 15
        z, x = a >> 2, a & 3
        half = t >> 1
        source = (x << 2) + z
        target = a
        mine, theirs = held
        away = (t & 1) ^ core
        write(jnp.where(away == 0, mine, SLOTS + theirs), k, half, source, half, target)
        return mine + 1 - away, theirs + away

    mine, theirs = lax.fori_loop(0, count, step, (jnp.int32(0), jnp.int32(0)))
    for i, n in enumerate((mine, theirs)):
        for g in range(GROUP):
            write(i * SLOTS + n + g, 0, 16, 0, 0, 16)
        groups[i] = (n + GROUP - 1) // GROUP


def entry(lists, which, field, j):
    return lists[field * 2 * SLOTS + which * SLOTS + j]


def forward_kernel(which, lists, groups, blocks, nodes, out, acc):
    acc[...] = jnp.zeros_like(acc)

    def step(i, _):
        products = []
        for g in range(GROUP):
            j = i * GROUP + g
            product = dot(blocks[entry(lists, which, 0, j)], nodes[entry(lists, which, 2, j)])
            products.append((entry(lists, which, 1, j), product))
        for slot, product in products:
            acc[slot] += product
        return 0

    lax.fori_loop(0, groups[which], step, 0)
    out[...] = acc[0:16].astype(BF)


def middle_kernel(info, parts, weight, cotangent, output, spread, stay, go, grad):
    total = parts[0].astype(F32)
    for s in range(1, 16):
        total += parts[s].astype(F32)
    share = total.astype(BF)
    pre = dot(share, weight[...])
    sigma = 1.0 / (1.0 + jnp.exp(-pre))
    output[...] = (pre * sigma).astype(BF)
    slope = sigma * (1.0 + pre * (1.0 - sigma))
    slopes = (cotangent[...].astype(F32) * slope).astype(BF)
    turned = slopes.astype(F32).T.astype(BF)
    for s in range(16):
        spread[s] = turned
    grad[...] = dot(share.astype(F32).T.astype(BF), slopes).reshape(2, 128, 256)
    stay[...] = grad[info[1]]
    go[...] = grad[1 - info[1]]


def scatter_kernel(me, count, info, *refs):
    parts, outs, scratch = refs[:count], refs[count:-1], refs[-1]
    total = parts[0][...]
    for part in parts[1:]:
        total += part[...]
    rows = total.shape[0] // 4
    for k in range(4):
        scratch[k] = total[rows * k : rows * k + rows]
    for k, out in enumerate(outs):
        out[...] = scratch[(info[me] + k) & 3]


def offer_kernel(w0, w1, w2, w3, own, out, held):
    total = w0[...] + w1[...] + w2[...] + w3[...]
    for s in range(16):
        out[s] = total


def back_products(which, lists, groups, blocks, source, acc):
    def step(i, _):
        products = []
        for g in range(GROUP):
            j = i * GROUP + g
            product = dot(source[entry(lists, which, 3, j)], blocks[entry(lists, which, 0, j)])
            products.append((entry(lists, which, 4, j), product))
        for slot, product in products:
            acc[slot] += product
        return 0

    lax.fori_loop(0, groups[which], step, 0)


def backward_own_kernel(lists, groups, blocks, own, acc):
    acc[...] = jnp.zeros_like(acc)
    back_products(0, lists, groups, blocks, own, acc)


def backward_other_kernel(scale, lists, groups, blocks, other, grads, begun, out, acc):
    back_products(1, lists, groups, blocks, other, acc)
    grad = grads[0]
    for s in range(1, 16):
        grad += grads[s]
    grad = grad * scale
    packed = jnp.concatenate([grad[:, 0:128], grad[:, 128:256]], axis=0).astype(BF)
    for s in range(16):
        out[s, 0:256, :] = acc[s].astype(BF)
        out[s, 256:272, :] = packed


def grad_kernel(parts, out):
    for z in range(4):
        for x in range(4):
            packed = parts[4 * z + x, 256:272, :].astype(F32)
            row = 32 * x + 8 * z
            out[row : row + 8, 0:128] = packed[0:8]
            out[row : row + 8, 128:256] = packed[8:16]


def last_kernel(parts, weight, input_grad):
    total = parts[0, 0:256, :].astype(F32)
    for s in range(1, 16):
        total += parts[s, 0:256, :].astype(F32)
    back = total.astype(BF).astype(F32).T.astype(BF)
    input_grad[...] = dot(back, weight[...], (((1,), (1,)), ((), ()))).astype(BF)


def join_kernel(info, mine, theirs, out):
    out[info[1]] = mine[...]
    out[1 - info[1]] = theirs[...]


def call(kernel, outs, kinds, scratch=(), flops=0, size=0, alias=None):
    return pl.pallas_call(
        kernel,
        out_shape=[jax.ShapeDtypeStruct(s, d) for s, d, _ in outs],
        in_specs=kinds,
        out_specs=[k for _, _, k in outs],
        scratch_shapes=list(scratch),
        input_output_aliases=alias or {},
        compiler_params=LIMIT,
        cost_estimate=pl.CostEstimate(flops=flops, bytes_accessed=size, transcendentals=0),
    )


def exchange(value, axes):
    return lax.all_to_all(value, axes, 0, 0, tiled=True)


def swap(value):
    return lax.ppermute(value, "c", [(0, 1), (1, 0)])


def rotate(value, axis, k):
    return lax.ppermute(value, axis, [(i, (i + k) % 4) for i in range(4)])


def shards(features, weight, cotangent, blocks, block_pos, counts):
    tile = blocks[0, 0]
    index = [lax.axis_index(a).astype(jnp.int32) for a in ("c", "x", "zl")]
    info = jnp.stack([counts[0, 0]] + index)
    nodes_total = 65536
    heavy = dict(flops=8 * 10**8, size=6 * 2**20)
    i32 = jnp.int32
    rounds = (1, 2, 3)

    lists, groups = call(
        plan_kernel,
        [((10 * SLOTS,), i32, SMEM), ((2,), i32, SMEM)],
        [SMEM, SMEM, VMEM],
        size=2**20,
    )(block_pos[0, 0], info, tile)

    line = exchange(jnp.broadcast_to(features[None], (4, 128, 256)), "zl")
    nodes = exchange(jnp.broadcast_to(line[None], (4, 4, 128, 256)), "x").reshape(16, 128, 256)
    send, keep = [
        call(
            functools.partial(forward_kernel, which),
            [((16, 128, 256), BF, VMEM)],
            [SMEM, SMEM, VMEM, VMEM],
            [pltpu.VMEM((17, 128, 256), F32)],
            **heavy,
        )(lists, groups, tile, nodes)[0]
        for which in (1, 0)
    ]
    pair = (keep.astype(F32) + swap(send).astype(F32)).astype(BF)
    parts = exchange(pair, ("zh", "y"))
    output, spread, stay, go = call(
        middle_kernel,
        [((128, 256), BF, VMEM), ((16, 256, 128), BF, VMEM)] + [((128, 256), F32, VMEM)] * 2,
        [SMEM, VMEM, VMEM, VMEM],
        [pltpu.VMEM((2, 128, 256), F32)],
    )(info, parts, weight, cotangent)
    own = exchange(spread, ("zh", "y"))

    def scatter(me, rows, held):
        return call(
            functools.partial(scatter_kernel, me, len(held)),
            [((rows, 256), F32, VMEM)] * 4,
            [SMEM] + [VMEM] * len(held),
            [pltpu.VMEM((4, rows, 256), F32)],
        )(info, *held)

    held = scatter(2, 32, [stay, swap(go)])
    held = scatter(3, 8, [held[0]] + [rotate(held[k], "x", k) for k in rounds])
    held = [held[0]] + [rotate(held[k], "zl", k) for k in rounds]
    offer, own = call(
        offer_kernel,
        [((16, 8, 256), F32, VMEM), ((16, 256, 128), BF, VMEM)],
        [VMEM] * 5,
        alias={4: 1},
    )(*held, own)
    grads = exchange(offer, ("zh", "y"))
    other = swap(own)
    (begun,) = call(
        backward_own_kernel,
        [((17, 256, 128), F32, VMEM)],
        [SMEM, SMEM, VMEM, VMEM],
        **heavy,
    )(lists, groups, tile, own)
    back, _ = call(
        functools.partial(backward_other_kernel, 1.0 / math.sqrt(nodes_total)),
        [((16, 272, 128), BF, VMEM), ((17, 256, 128), F32, VMEM)],
        [SMEM, SMEM] + [VMEM] * 4,
        alias={5: 1},
        **heavy,
    )(lists, groups, tile, other, grads, begun)
    parts = exchange(back, ("zl", "x"))
    (mine,) = call(grad_kernel, [((128, 256), F32, VMEM)], [VMEM])(parts)
    theirs = swap(mine)
    (input_grad,) = call(last_kernel, [((128, 256), BF, VMEM)], [VMEM] * 2, flops=2**24, size=2**20)(parts, weight)
    (weight_grad,) = call(join_kernel, [((2, 128, 256), F32, VMEM)], [SMEM, VMEM, VMEM])(info, mine, theirs)
    weight_grad = weight_grad.reshape(256, 256)
    return (output, input_grad, weight_grad)


def solution(mesh):
    names = ("zl", "x", "zh", "y", "c")
    row, col = names[:2], names[2:]
    fine = Mesh(mesh.devices.reshape(4, 4, 2, 8, 2), names)
    return jax.shard_map(
        shards,
        mesh=fine,
        in_specs=(
            P(col + row, None),
            P(),
            P(row + col, None),
            P(row, col, None, None, None),
            P(row, col, None),
            P(row, col),
        ),
        out_specs=(P(row + col, None), P(col + row, None), P()),
        check_vma=False,
    )
```

```python
import functools
import math

import jax
import jax.numpy as jnp
from jax import lax
from jax.experimental import pallas as pl
from jax.experimental.pallas import tpu as pltpu
from jax.sharding import Mesh
from jax.sharding import PartitionSpec as P

BF = jnp.bfloat16
F32 = jnp.float32
GROUP = 16
SLOTS = 112
VMEM = pl.BlockSpec(memory_space=pltpu.VMEM)
SMEM = pl.BlockSpec(memory_space=pltpu.SMEM)
LIMIT = pltpu.CompilerParams(vmem_limit_bytes=48 * 1024 * 1024)


def dot(a, b, dims=(((1,), (0,)), ((), ()))):
    return lax.dot_general(a, b, dims, preferred_element_type=F32)


def plan_kernel(place, info, blocks, lists, groups):
    count, core = info[0], info[1]

    def write(at, k, t, source, half, target):
        for f, value in enumerate((k, t, source, half, target)):
            lists[f * 2 * SLOTS + at] = value

    def step(k, held):
        p = place[k]
        t, a = p >> 4, p & 15
        z, x = a >> 2, a & 3
        half = t >> 1
        source = (x << 2) + z
        target = a
        mine, theirs = held
        away = (t & 1) ^ core
        write(jnp.where(away == 0, mine, SLOTS + theirs), k, half, source, half, target)
        return mine + 1 - away, theirs + away

    mine, theirs = lax.fori_loop(0, count, step, (jnp.int32(0), jnp.int32(0)))
    for i, n in enumerate((mine, theirs)):
        for g in range(GROUP):
            write(i * SLOTS + n + g, 0, 16, 0, 0, 16)
        groups[i] = (n + GROUP - 1) // GROUP


def entry(lists, which, field, j):
    return lists[field * 2 * SLOTS + which * SLOTS + j]


def forward_kernel(which, lists, groups, blocks, nodes, out, acc):
    acc[...] = jnp.zeros_like(acc)

    def step(i, _):
        products = []
        for g in range(GROUP):
            j = i * GROUP + g
            product = dot(blocks[entry(lists, which, 0, j)], nodes[entry(lists, which, 2, j)])
            products.append((entry(lists, which, 1, j), product))
        for slot, product in products:
            acc[slot] += product
        return 0

    lax.fori_loop(0, groups[which], step, 0)
    out[...] = acc[0:16].astype(BF)


def middle_kernel(parts, weight, cotangent, output, spread, turned_share, slopes_out):
    total = parts[0].astype(F32)
    for s in range(1, 16):
        total += parts[s].astype(F32)
    share = total.astype(BF)
    pre = dot(share, weight[...])
    sigma = 1.0 / (1.0 + jnp.exp(-pre))
    output[...] = (pre * sigma).astype(BF)
    slope = sigma * (1.0 + pre * (1.0 - sigma))
    slopes = (cotangent[...].astype(F32) * slope).astype(BF)
    turned = slopes.astype(F32).T.astype(BF)
    for s in range(16):
        spread[s] = turned
    turned_share[...] = share.astype(F32).T.astype(BF)
    slopes_out[...] = slopes


def product_kernel(info, turned_share, slopes, stay, go, grad):
    grad[...] = dot(turned_share[...], slopes[...]).reshape(2, 128, 256)
    stay[...] = grad[info[1]]
    go[...] = grad[1 - info[1]]


def scatter_kernel(me, count, info, *refs):
    parts, outs, scratch = refs[:count], refs[count:-1], refs[-1]
    total = parts[0][...]
    for part in parts[1:]:
        total += part[...]
    rows = total.shape[0] // 4
    for k in range(4):
        scratch[k] = total[rows * k : rows * k + rows]
    for k, out in enumerate(outs):
        out[...] = scratch[(info[me] + k) & 3]


def gate_kernel(mine, theirs, own, out, held):
    out[...] = mine[...] + theirs[...]


def back_products(which, lists, groups, blocks, source, acc):
    def step(i, _):
        products = []
        for g in range(GROUP):
            j = i * GROUP + g
            product = dot(source[entry(lists, which, 3, j)], blocks[entry(lists, which, 0, j)])
            products.append((entry(lists, which, 4, j), product))
        for slot, product in products:
            acc[slot] += product
        return 0

    lax.fori_loop(0, groups[which], step, 0)


def backward_own_kernel(lists, groups, blocks, own, acc):
    acc[...] = jnp.zeros_like(acc)
    back_products(0, lists, groups, blocks, own, acc)


def backward_other_kernel(lists, groups, blocks, other, mine, theirs, begun, out, total, acc):
    total[...] = mine[...] + theirs[...]
    back_products(1, lists, groups, blocks, other, acc)
    out[...] = acc[0:16].astype(BF)


def gather_kernel(scale, info, w0, w1, w2, w3, parts, out, held):
    for k, part in enumerate((w0, w1, w2, w3)):
        out[(info[2] - k) & 3] = part[...] * scale


def last_kernel(parts, weight, input_grad):
    total = parts[0].astype(F32)
    for s in range(1, 16):
        total += parts[s].astype(F32)
    back = total.astype(BF).astype(F32).T.astype(BF)
    input_grad[...] = dot(back, weight[...], (((1,), (1,)), ((), ()))).astype(BF)


def join_kernel(info, mine, theirs, out):
    out[info[1]] = mine[...]
    out[1 - info[1]] = theirs[...]


def call(kernel, outs, kinds, scratch=(), flops=0, size=0, alias=None):
    return pl.pallas_call(
        kernel,
        out_shape=[jax.ShapeDtypeStruct(s, d) for s, d, _ in outs],
        in_specs=kinds,
        out_specs=[k for _, _, k in outs],
        scratch_shapes=list(scratch),
        input_output_aliases=alias or {},
        compiler_params=LIMIT,
        cost_estimate=pl.CostEstimate(flops=flops, bytes_accessed=size, transcendentals=0),
    )


def exchange(value, axes):
    return lax.all_to_all(value, axes, 0, 0, tiled=True)


def swap(value):
    return lax.ppermute(value, "c", [(0, 1), (1, 0)])


def paired_sum(value, axis, size, k):
    return value + lax.ppermute(value, axis, [(i, i ^ k) for i in range(size)])


def rotate(value, axis, k):
    return lax.ppermute(value, axis, [(i, (i + k) % 4) for i in range(4)])


def shards(features, weight, cotangent, blocks, block_pos, counts):
    tile = blocks[0, 0]
    index = [lax.axis_index(a).astype(jnp.int32) for a in ("c", "x", "zl")]
    info = jnp.stack([counts[0, 0]] + index)
    nodes_total = 65536
    heavy = dict(flops=8 * 10**8, size=6 * 2**20)
    i32 = jnp.int32
    rounds = (1, 2, 3)

    lists, groups = call(
        plan_kernel,
        [((10 * SLOTS,), i32, SMEM), ((2,), i32, SMEM)],
        [SMEM, SMEM, VMEM],
        size=2**20,
    )(block_pos[0, 0], info, tile)

    line = exchange(jnp.broadcast_to(features[None], (4, 128, 256)), "zl")
    nodes = exchange(jnp.broadcast_to(line[None], (4, 4, 128, 256)), "x").reshape(16, 128, 256)
    send, keep = [
        call(
            functools.partial(forward_kernel, which),
            [((16, 128, 256), BF, VMEM)],
            [SMEM, SMEM, VMEM, VMEM],
            [pltpu.VMEM((17, 128, 256), F32)],
            **heavy,
        )(lists, groups, tile, nodes)[0]
        for which in (1, 0)
    ]
    pair = (keep.astype(F32) + swap(send).astype(F32)).astype(BF)
    parts = exchange(pair, ("zh", "y"))
    output, spread, share, slopes = call(
        middle_kernel,
        [((128, 256), BF, VMEM), ((16, 256, 128), BF, VMEM), ((256, 128), BF, VMEM), ((128, 256), BF, VMEM)],
        [VMEM, VMEM, VMEM],
    )(parts, weight, cotangent)
    own = exchange(spread, ("zh", "y"))

    stay, go = call(
        product_kernel,
        [((128, 256), F32, VMEM)] * 2,
        [SMEM, VMEM, VMEM],
        [pltpu.VMEM((2, 128, 256), F32)],
    )(info, share, slopes)
    held = call(
        functools.partial(scatter_kernel, 2, 2),
        [((32, 256), F32, VMEM)] * 4,
        [SMEM, VMEM, VMEM],
        [pltpu.VMEM((4, 32, 256), F32)],
    )(info, stay, swap(go))
    held = [held[0]] + [rotate(held[k], "x", k) for k in rounds]
    total = paired_sum(held[0] + held[1] + held[2] + held[3], "zh", 2, 1)
    total, own = call(
        gate_kernel,
        [((32, 256), F32, VMEM), ((16, 256, 128), BF, VMEM)],
        [VMEM] * 3,
        alias={2: 1},
    )(total, lax.ppermute(total, "y", [(i, i ^ 1) for i in range(8)]), own)
    other = swap(own)
    (begun,) = call(
        backward_own_kernel,
        [((17, 256, 128), F32, VMEM)],
        [SMEM, SMEM, VMEM, VMEM],
        **heavy,
    )(lists, groups, tile, own)
    theirs = lax.ppermute(total, "y", [(i, i ^ 2) for i in range(8)])
    back, total, _ = call(
        backward_other_kernel,
        [((16, 256, 128), BF, VMEM), ((32, 256), F32, VMEM), ((17, 256, 128), F32, VMEM)],
        [SMEM, SMEM] + [VMEM] * 5,
        alias={6: 2},
        **heavy,
    )(lists, groups, tile, other, total, theirs, begun)
    total = paired_sum(total, "y", 8, 4)
    total = paired_sum(paired_sum(total, "zl", 4, 1), "zl", 4, 2)
    parts = exchange(back, ("zl", "x"))
    mine, parts = call(
        functools.partial(gather_kernel, 1.0 / math.sqrt(nodes_total)),
        [((4, 32, 256), F32, VMEM), ((16, 256, 128), BF, VMEM)],
        [SMEM] + [VMEM] * 5,
        alias={5: 1},
    )(info, total, *[rotate(total, "x", k) for k in rounds], parts)
    theirs = swap(mine)
    (input_grad,) = call(last_kernel, [((128, 256), BF, VMEM)], [VMEM] * 2, flops=2**24, size=2**20)(parts, weight)
    (weight_grad,) = call(join_kernel, [((2, 4, 32, 256), F32, VMEM)], [SMEM, VMEM, VMEM])(info, mine, theirs)
    weight_grad = weight_grad.reshape(256, 256)
    return (output, input_grad, weight_grad)


def solution(mesh):
    names = ("zl", "x", "zh", "y", "c")
    row, col = names[:2], names[2:]
    fine = Mesh(mesh.devices.reshape(4, 4, 2, 8, 2), names)
    return jax.shard_map(
        shards,
        mesh=fine,
        in_specs=(
            P(col + row, None),
            P(),
            P(row + col, None),
            P(row, col, None, None, None),
            P(row, col, None),
            P(row, col),
        ),
        out_specs=(P(row + col, None), P(col + row, None), P()),
        check_vma=False,
    )
```

```python
import functools
import math

import jax
import jax.numpy as jnp
from jax import lax
from jax.experimental import pallas as pl
from jax.experimental.pallas import tpu as pltpu
from jax.sharding import Mesh
from jax.sharding import PartitionSpec as P

BF = jnp.bfloat16
F32 = jnp.float32
GROUP = 16
SLOTS = 112
VMEM = pl.BlockSpec(memory_space=pltpu.VMEM)
SMEM = pl.BlockSpec(memory_space=pltpu.SMEM)
LIMIT = pltpu.CompilerParams(vmem_limit_bytes=48 * 1024 * 1024)


def dot(a, b, dims=(((1,), (0,)), ((), ()))):
    return lax.dot_general(a, b, dims, preferred_element_type=F32)


def plan_kernel(place, info, blocks, lists, groups):
    count, core = info[0], info[1]

    def write(at, k, t, source, half, target):
        for f, value in enumerate((k, t, source, half, target)):
            lists[f * 2 * SLOTS + at] = value

    def step(k, held):
        p = place[k]
        t, a = p >> 4, p & 15
        z, x = a >> 2, a & 3
        half = t >> 1
        source = (x << 2) + z
        target = a
        mine, theirs = held
        away = (t & 1) ^ core
        write(jnp.where(away == 0, mine, SLOTS + theirs), k, half, source, half, target)
        return mine + 1 - away, theirs + away

    mine, theirs = lax.fori_loop(0, count, step, (jnp.int32(0), jnp.int32(0)))
    for i, n in enumerate((mine, theirs)):
        for g in range(GROUP):
            write(i * SLOTS + n + g, 0, 16, 0, 0, 16)
        groups[i] = (n + GROUP - 1) // GROUP


def entry(lists, which, field, j):
    return lists[field * 2 * SLOTS + which * SLOTS + j]


def forward_kernel(which, lists, groups, blocks, nodes, out, acc):
    acc[...] = jnp.zeros_like(acc)

    def step(i, _):
        products = []
        for g in range(GROUP):
            j = i * GROUP + g
            product = dot(blocks[entry(lists, which, 0, j)], nodes[entry(lists, which, 2, j)])
            products.append((entry(lists, which, 1, j), product))
        for slot, product in products:
            acc[slot] += product
        return 0

    lax.fori_loop(0, groups[which], step, 0)
    out[...] = acc[0:16].astype(BF)


def middle_kernel(parts, weight, cotangent, output, spread):
    total = parts[0].astype(F32)
    for s in range(1, 16):
        total += parts[s].astype(F32)
    share = total.astype(BF)
    pre = dot(share, weight[...])
    sigma = 1.0 / (1.0 + jnp.exp(-pre))
    output[...] = (pre * sigma).astype(BF)
    slope = sigma * (1.0 + pre * (1.0 - sigma))
    slopes32 = cotangent[...].astype(F32) * slope
    slopes = slopes32.astype(BF)
    turned = slopes.astype(F32).T.astype(BF)
    grad = dot(share.astype(F32).T.astype(BF), slopes).astype(BF)
    for s in range(16):
        spread[s, 0:256, :] = turned
        rows = slice(32 * (s % 8), 32 * (s % 8) + 32)
        spread[s, 256:288, :] = grad[rows, 0:128]
        spread[s, 288:320, :] = grad[rows, 128:256]


def back_products(which, lists, groups, blocks, source, acc):
    def step(i, _):
        products = []
        for g in range(GROUP):
            j = i * GROUP + g
            product = dot(source[entry(lists, which, 3, j), 0:256, :], blocks[entry(lists, which, 0, j)])
            products.append((entry(lists, which, 4, j), product))
        for slot, product in products:
            acc[slot] += product
        return 0

    lax.fori_loop(0, groups[which], step, 0)


def backward_own_kernel(lists, groups, blocks, own, acc):
    acc[...] = jnp.zeros_like(acc)
    back_products(0, lists, groups, blocks, own, acc)


def backward_other_kernel(lists, groups, blocks, own, other, begun, out, grad_out, acc):
    back_products(1, lists, groups, blocks, other, acc)
    out[...] = acc[0:16].astype(BF)
    grad = jnp.zeros((64, 128), F32)
    for s in range(16):
        grad += own[s, 256:320, :].astype(F32) + other[s, 256:320, :].astype(F32)
    grad_out[...] = grad


def gate_kernel(scale, total, parts, out, held):
    grad = (total[...] * scale).astype(BF)
    for s in range(8):
        out[s, :, 0:128] = grad[0:32]
        out[s, :, 128:256] = grad[32:64]


def last_kernel(parts, weight, input_grad):
    total = parts[0].astype(F32)
    for s in range(1, 16):
        total += parts[s].astype(F32)
    back = total.astype(BF).astype(F32).T.astype(BF)
    input_grad[...] = dot(back, weight[...], (((1,), (1,)), ((), ()))).astype(BF)


def call(kernel, outs, kinds, scratch=(), flops=0, size=0, alias=None):
    return pl.pallas_call(
        kernel,
        out_shape=[jax.ShapeDtypeStruct(s, d) for s, d, _ in outs],
        in_specs=kinds,
        out_specs=[k for _, _, k in outs],
        scratch_shapes=list(scratch),
        input_output_aliases=alias or {},
        compiler_params=LIMIT,
        cost_estimate=pl.CostEstimate(flops=flops, bytes_accessed=size, transcendentals=0),
    )


def exchange(value, axes):
    return lax.all_to_all(value, axes, 0, 0, tiled=True)


def swap(value):
    return lax.ppermute(value, "c", [(0, 1), (1, 0)])


def paired_sum(value, axis, k):
    return value + lax.ppermute(value, axis, [(i, i ^ k) for i in range(4)])


def shards(features, weight, cotangent, blocks, block_pos, counts):
    tile = blocks[0, 0]
    index = [lax.axis_index(a).astype(jnp.int32) for a in ("c", "x", "zl")]
    info = jnp.stack([counts[0, 0]] + index)
    nodes_total = 65536
    heavy = dict(flops=8 * 10**8, size=6 * 2**20)
    i32 = jnp.int32

    lists, groups = call(
        plan_kernel,
        [((10 * SLOTS,), i32, SMEM), ((2,), i32, SMEM)],
        [SMEM, SMEM, VMEM],
        size=2**20,
    )(block_pos[0, 0], info, tile)

    line = exchange(jnp.broadcast_to(features[None], (4, 128, 256)), "zl")
    nodes = exchange(jnp.broadcast_to(line[None], (4, 4, 128, 256)), "x").reshape(16, 128, 256)
    send, keep = [
        call(
            functools.partial(forward_kernel, which),
            [((16, 128, 256), BF, VMEM)],
            [SMEM, SMEM, VMEM, VMEM],
            [pltpu.VMEM((17, 128, 256), F32)],
            **heavy,
        )(lists, groups, tile, nodes)[0]
        for which in (1, 0)
    ]
    pair = (keep.astype(F32) + swap(send).astype(F32)).astype(BF)
    parts = exchange(pair, ("zh", "y"))
    output, spread = call(
        middle_kernel,
        [((128, 256), BF, VMEM), ((16, 320, 128), BF, VMEM)],
        [VMEM, VMEM, VMEM],
    )(parts, weight, cotangent)
    own = exchange(spread, ("zh", "y"))
    other = swap(own)
    (begun,) = call(
        backward_own_kernel,
        [((17, 256, 128), F32, VMEM)],
        [SMEM, SMEM, VMEM, VMEM],
        **heavy,
    )(lists, groups, tile, own)
    back, total, _ = call(
        backward_other_kernel,
        [((16, 256, 128), BF, VMEM), ((64, 128), F32, VMEM), ((17, 256, 128), F32, VMEM)],
        [SMEM, SMEM] + [VMEM] * 4,
        alias={5: 2},
        **heavy,
    )(lists, groups, tile, own, other, begun)
    parts = exchange(back, ("zl", "x"))
    for axis in ("x", "zl"):
        total = paired_sum(paired_sum(total, axis, 1), axis, 2)
    grad, parts = call(
        functools.partial(gate_kernel, 1.0 / math.sqrt(nodes_total)),
        [((8, 32, 256), BF, VMEM), ((16, 256, 128), BF, VMEM)],
        [VMEM, VMEM],
        alias={1: 1},
    )(total, parts)
    weight_grad = exchange(grad, "y").reshape(256, 256).astype(F32)
    (input_grad,) = call(last_kernel, [((128, 256), BF, VMEM)], [VMEM] * 2, flops=2**24, size=2**20)(parts, weight)
    return (output, input_grad, weight_grad)


def solution(mesh):
    names = ("zl", "x", "zh", "y", "c")
    row, col = names[:2], names[2:]
    fine = Mesh(mesh.devices.reshape(4, 4, 2, 8, 2), names)
    return jax.shard_map(
        shards,
        mesh=fine,
        in_specs=(
            P(col + row, None),
            P(),
            P(row + col, None),
            P(row, col, None, None, None),
            P(row, col, None),
            P(row, col),
        ),
        out_specs=(P(row + col, None), P(col + row, None), P()),
        check_vma=False,
    )
```

```python
import functools
import math

import jax
import jax.numpy as jnp
from jax import lax
from jax.experimental import pallas as pl
from jax.experimental.pallas import tpu as pltpu
from jax.sharding import Mesh
from jax.sharding import PartitionSpec as P

BF = jnp.bfloat16
F32 = jnp.float32
GROUP = 16
SLOTS = 112
VMEM = pl.BlockSpec(memory_space=pltpu.VMEM)
SMEM = pl.BlockSpec(memory_space=pltpu.SMEM)
LIMIT = pltpu.CompilerParams(vmem_limit_bytes=48 * 1024 * 1024)


def dot(a, b, dims=(((1,), (0,)), ((), ()))):
    return lax.dot_general(a, b, dims, preferred_element_type=F32)


def plan_kernel(place, info, blocks, lists, groups):
    count, core = info[0], info[1]

    def write(at, k, t, source, half, target):
        for f, value in enumerate((k, t, source, half, target)):
            lists[f * 2 * SLOTS + at] = value

    def step(k, held):
        p = place[k]
        t, a = p >> 4, p & 15
        half = t >> 1
        mine, theirs = held
        away = (t & 1) ^ core
        write(jnp.where(away == 0, mine, SLOTS + theirs), k, half, a, half, a)
        return mine + 1 - away, theirs + away

    mine, theirs = lax.fori_loop(0, count, step, (jnp.int32(0), jnp.int32(0)))
    for i, n in enumerate((mine, theirs)):
        for g in range(GROUP):
            write(i * SLOTS + n + g, 0, 16, 0, 0, 16)
        groups[i] = (n + GROUP - 1) // GROUP


def entry(lists, which, field, j):
    return lists[field * 2 * SLOTS + which * SLOTS + j]


def forward_kernel(which, lists, groups, blocks, nodes, out, acc):
    acc[...] = jnp.zeros_like(acc)

    def step(i, _):
        products = []
        for g in range(GROUP):
            j = i * GROUP + g
            product = dot(blocks[entry(lists, which, 0, j)], nodes[entry(lists, which, 2, j)])
            products.append((entry(lists, which, 1, j), product))
        for slot, product in products:
            acc[slot] += product
        return 0

    lax.fori_loop(0, groups[which], step, 0)
    out[...] = acc[0:16].astype(BF)


def middle_kernel(parts, weight, cotangent, output, spread):
    total = parts[0].astype(F32)
    for s in range(1, 16):
        total += parts[s].astype(F32)
    share = total.astype(BF)
    pre = dot(share, weight[...])
    sigma = 1.0 / (1.0 + jnp.exp(-pre))
    output[...] = (pre * sigma).astype(BF)
    slope = sigma * (1.0 + pre * (1.0 - sigma))
    slopes32 = cotangent[...].astype(F32) * slope
    slopes = slopes32.astype(BF)
    turned = slopes.astype(F32).T.astype(BF)
    grad = dot(share.astype(F32).T.astype(BF), slopes).astype(BF)
    for s in range(16):
        spread[s, 0:256, :] = turned
        rows = slice(32 * (s % 8), 32 * (s % 8) + 32)
        spread[s, 256:288, :] = grad[rows, 0:128]
        spread[s, 288:320, :] = grad[rows, 128:256]


def back_products(which, lists, groups, blocks, source, acc):
    def step(i, _):
        products = []
        for g in range(GROUP):
            j = i * GROUP + g
            product = dot(source[entry(lists, which, 3, j), 0:256, :], blocks[entry(lists, which, 0, j)])
            products.append((entry(lists, which, 4, j), product))
        for slot, product in products:
            acc[slot] += product
        return 0

    lax.fori_loop(0, groups[which], step, 0)


def backward_own_kernel(lists, groups, blocks, own, acc, grad_out):
    grad = own[0, 256:320, :].astype(F32)
    for s in range(1, 16):
        grad += own[s, 256:320, :].astype(F32)
    grad_out[...] = grad
    acc[...] = jnp.zeros_like(acc)
    back_products(0, lists, groups, blocks, own, acc)


def backward_other_kernel(lists, groups, blocks, other, mine, theirs, begun, out, total, acc):
    total[...] = mine[...] + theirs[...]
    back_products(1, lists, groups, blocks, other, acc)
    out[...] = acc[0:16].astype(BF)


def gate_kernel(scale, total, parts, out, held):
    grad = (total[...] * scale).astype(BF)
    for s in range(8):
        out[s, :, 0:128] = grad[0:32]
        out[s, :, 128:256] = grad[32:64]


def last_kernel(parts, weight, input_grad):
    total = parts[0].astype(F32)
    for s in range(1, 16):
        total += parts[s].astype(F32)
    back = total.astype(BF).astype(F32).T.astype(BF)
    input_grad[...] = dot(back, weight[...], (((1,), (1,)), ((), ()))).astype(BF)


def call(kernel, outs, kinds, scratch=(), flops=0, size=0, alias=None):
    return pl.pallas_call(
        kernel,
        out_shape=[jax.ShapeDtypeStruct(s, d) for s, d, _ in outs],
        in_specs=kinds,
        out_specs=[k for _, _, k in outs],
        scratch_shapes=list(scratch),
        input_output_aliases=alias or {},
        compiler_params=LIMIT,
        cost_estimate=pl.CostEstimate(flops=flops, bytes_accessed=size, transcendentals=0),
    )


def exchange(value, axes):
    return lax.all_to_all(value, axes, 0, 0, tiled=True)


def swap(value):
    return lax.ppermute(value, "c", [(0, 1), (1, 0)])


def paired(value, axis, k):
    return lax.ppermute(value, axis, [(i, i ^ k) for i in range(4)])


def shards(features, weight, cotangent, blocks, block_pos, counts):
    tile = blocks[0, 0]
    index = [lax.axis_index(a).astype(jnp.int32) for a in ("c", "x", "zl")]
    info = jnp.stack([counts[0, 0]] + index)
    nodes_total = 65536
    heavy = dict(flops=8 * 10**8, size=6 * 2**20)
    i32 = jnp.int32

    lists, groups = call(
        plan_kernel,
        [((10 * SLOTS,), i32, SMEM), ((2,), i32, SMEM)],
        [SMEM, SMEM, VMEM],
        size=2**20,
    )(block_pos[0, 0], info, tile)

    nodes = exchange(jnp.broadcast_to(features[None], (16, 128, 256)), ("zl", "x"))
    send, keep = [
        call(
            functools.partial(forward_kernel, which),
            [((16, 128, 256), BF, VMEM)],
            [SMEM, SMEM, VMEM, VMEM],
            [pltpu.VMEM((17, 128, 256), F32)],
            **heavy,
        )(lists, groups, tile, nodes)[0]
        for which in (1, 0)
    ]
    pair = (keep.astype(F32) + swap(send).astype(F32)).astype(BF)
    parts = exchange(pair, ("zh", "y"))
    output, spread = call(
        middle_kernel,
        [((128, 256), BF, VMEM), ((16, 320, 128), BF, VMEM)],
        [VMEM, VMEM, VMEM],
    )(parts, weight, cotangent)
    own = exchange(spread, ("zh", "y"))
    other = swap(own)
    begun, total = call(
        backward_own_kernel,
        [((17, 256, 128), F32, VMEM), ((64, 128), F32, VMEM)],
        [SMEM, SMEM, VMEM, VMEM],
        **heavy,
    )(lists, groups, tile, own)
    back, total, _ = call(
        backward_other_kernel,
        [((16, 256, 128), BF, VMEM), ((64, 128), F32, VMEM), ((17, 256, 128), F32, VMEM)],
        [SMEM, SMEM] + [VMEM] * 5,
        alias={6: 2},
        **heavy,
    )(lists, groups, tile, other, total, paired(total, "x", 1), begun)
    parts = exchange(back, ("zl", "x"))
    for axis, k in (("x", 2), ("zl", 1), ("zl", 2)):
        total = total + paired(total, axis, k)
    total = total + swap(total)
    grad, parts = call(
        functools.partial(gate_kernel, 1.0 / math.sqrt(nodes_total)),
        [((8, 32, 256), BF, VMEM), ((16, 256, 128), BF, VMEM)],
        [VMEM, VMEM],
        alias={1: 1},
    )(total, parts)
    weight_grad = exchange(grad, "y").reshape(256, 256).astype(F32)
    (input_grad,) = call(last_kernel, [((128, 256), BF, VMEM)], [VMEM] * 2, flops=2**24, size=2**20)(parts, weight)
    return (output, input_grad, weight_grad)


def solution(mesh):
    names = ("zl", "x", "zh", "y", "c")
    row, col = names[:2], names[2:]
    fine = Mesh(mesh.devices.reshape(4, 4, 2, 8, 2), names)
    return jax.shard_map(
        shards,
        mesh=fine,
        in_specs=(
            P(col + row, None),
            P(),
            P(row + col, None),
            P(row, col, None, None, None),
            P(row, col, None),
            P(row, col),
        ),
        out_specs=(P(row + col, None), P(col + row, None), P()),
        check_vma=False,
    )
```

```python
import functools
import math

import jax
import jax.numpy as jnp
from jax import lax
from jax.experimental import pallas as pl
from jax.experimental.pallas import tpu as pltpu
from jax.sharding import Mesh
from jax.sharding import PartitionSpec as P

BF = jnp.bfloat16
F32 = jnp.float32
GROUP = 16
SLOTS = 112
VMEM = pl.BlockSpec(memory_space=pltpu.VMEM)
SMEM = pl.BlockSpec(memory_space=pltpu.SMEM)
LIMIT = pltpu.CompilerParams(vmem_limit_bytes=48 * 1024 * 1024)


def dot(a, b, dims=(((1,), (0,)), ((), ()))):
    return lax.dot_general(a, b, dims, preferred_element_type=F32)


def plan_kernel(place, info, blocks, lists, groups):
    count, core, zi = info[0], info[1], info[2]

    def write(at, k, t, source, half, target):
        for f, value in enumerate((k, t, source, half, target)):
            lists[f * 2 * SLOTS + at] = value

    def step(k, held):
        p = place[k]
        t, a = p >> 4, p & 15
        z, x = a >> 2, a & 3
        half = t >> 1
        source = (x << 2) + z
        target = (x << 2) + ((z - zi) & 3)
        mine, theirs = held
        away = (t & 1) ^ core
        write(jnp.where(away == 0, mine, SLOTS + theirs), k, half, source, half, target)
        return mine + 1 - away, theirs + away

    mine, theirs = lax.fori_loop(0, count, step, (jnp.int32(0), jnp.int32(0)))
    for i, n in enumerate((mine, theirs)):
        for g in range(GROUP):
            write(i * SLOTS + n + g, 0, 16, 0, 0, 16)
        groups[i] = (n + GROUP - 1) // GROUP


def entry(lists, which, field, j):
    return lists[field * 2 * SLOTS + which * SLOTS + j]


def forward_kernel(which, lists, groups, blocks, nodes, out, acc):
    acc[...] = jnp.zeros_like(acc)

    def step(i, _):
        products = []
        for g in range(GROUP):
            j = i * GROUP + g
            product = dot(blocks[entry(lists, which, 0, j)], nodes[entry(lists, which, 2, j)])
            products.append((entry(lists, which, 1, j), product))
        for slot, product in products:
            acc[slot] += product
        return 0

    lax.fori_loop(0, groups[which], step, 0)
    out[...] = acc[0:16].astype(BF)


def middle_kernel(parts, weight, cotangent, output, spread):
    total = parts[0].astype(F32)
    for s in range(1, 16):
        total += parts[s].astype(F32)
    share = total.astype(BF)
    pre = dot(share, weight[...])
    sigma = 1.0 / (1.0 + jnp.exp(-pre))
    output[...] = (pre * sigma).astype(BF)
    slope = sigma * (1.0 + pre * (1.0 - sigma))
    slopes32 = cotangent[...].astype(F32) * slope
    slopes = slopes32.astype(BF)
    turned = slopes.astype(F32).T.astype(BF)
    grad = dot(share.astype(F32).T.astype(BF), slopes).astype(BF)
    for s in range(16):
        spread[s, 0:256, :] = turned
        rows = slice(32 * (s % 8), 32 * (s % 8) + 32)
        spread[s, 256:288, :] = grad[rows, 0:128]
        spread[s, 288:320, :] = grad[rows, 128:256]


def back_products(which, lists, groups, blocks, source, acc):
    def step(i, _):
        products = []
        for g in range(GROUP):
            j = i * GROUP + g
            product = dot(source[entry(lists, which, 3, j), 0:256, :], blocks[entry(lists, which, 0, j)])
            products.append((entry(lists, which, 4, j), product))
        for slot, product in products:
            acc[slot] += product
        return 0

    lax.fori_loop(0, groups[which], step, 0)


def backward_own_kernel(lists, groups, blocks, own, acc):
    acc[...] = jnp.zeros_like(acc)
    back_products(0, lists, groups, blocks, own, acc)


def backward_other_kernel(lists, groups, blocks, own, other, begun, out, acc):
    back_products(1, lists, groups, blocks, other, acc)
    grad = jnp.zeros((64, 128), F32)
    for s in range(16):
        grad += own[s, 256:320, :].astype(F32) + other[s, 256:320, :].astype(F32)
    grad = grad.astype(BF)
    for x in range(4):
        for z in range(4):
            out[x, 256 * z : 256 * z + 256, :] = acc[4 * x + z].astype(BF)
        out[x, 1024:1088, :] = grad


def fold_kernel(parts, f0, f1, f2, f3):
    grad = parts[0, 1024:1088, :].astype(F32)
    for x in range(1, 4):
        grad += parts[x, 1024:1088, :].astype(F32)
    grad = grad.astype(BF)
    for z, out in enumerate((f0, f1, f2, f3)):
        rows = slice(256 * z, 256 * z + 256)
        total = parts[0, rows, :].astype(F32)
        for x in range(1, 4):
            total += parts[x, rows, :].astype(F32)
        out[0:256, :] = total.astype(BF)
        out[256:320, :] = grad


def grad_kernel(scale, info, f0, f1, f2, f3, grad_out, scratch):
    for k, part in enumerate((f0, f1, f2, f3)):
        scratch[(info[2] - k) & 3] = part[256:320, :].astype(F32)
    grad = ((scratch[0] + scratch[1] + scratch[2] + scratch[3]) * scale).astype(BF)
    for s in range(8):
        grad_out[s, :, 0:128] = grad[0:32]
        grad_out[s, :, 128:256] = grad[32:64]


def last_kernel(f0, f1, f2, f3, weight, input_grad):
    total = f0[0:256, :].astype(F32)
    for part in (f1, f2, f3):
        total += part[0:256, :].astype(F32)
    back = total.astype(BF).astype(F32).T.astype(BF)
    input_grad[...] = dot(back, weight[...], (((1,), (1,)), ((), ()))).astype(BF)


def call(kernel, outs, kinds, scratch=(), flops=0, size=0, alias=None):
    return pl.pallas_call(
        kernel,
        out_shape=[jax.ShapeDtypeStruct(s, d) for s, d, _ in outs],
        in_specs=kinds,
        out_specs=[k for _, _, k in outs],
        scratch_shapes=list(scratch),
        input_output_aliases=alias or {},
        compiler_params=LIMIT,
        cost_estimate=pl.CostEstimate(flops=flops, bytes_accessed=size, transcendentals=0),
    )


def exchange(value, axes):
    return lax.all_to_all(value, axes, 0, 0, tiled=True)


def swap(value):
    return lax.ppermute(value, "c", [(0, 1), (1, 0)])


def rotate(value, axis, k):
    return lax.ppermute(value, axis, [(i, (i + k) % 4) for i in range(4)])


def shards(features, weight, cotangent, blocks, block_pos, counts):
    tile = blocks[0, 0]
    index = [lax.axis_index(a).astype(jnp.int32) for a in ("c", "zl")]
    info = jnp.stack([counts[0, 0]] + index)
    nodes_total = 65536
    heavy = dict(flops=8 * 10**8, size=6 * 2**20)
    i32 = jnp.int32

    lists, groups = call(
        plan_kernel,
        [((10 * SLOTS,), i32, SMEM), ((2,), i32, SMEM)],
        [SMEM, SMEM, VMEM],
        size=2**20,
    )(block_pos[0, 0], info, tile)

    line = exchange(jnp.broadcast_to(features[None], (4, 128, 256)), "zl")
    nodes = exchange(jnp.broadcast_to(line[None], (4, 4, 128, 256)), "x").reshape(16, 128, 256)
    send, keep = [
        call(
            functools.partial(forward_kernel, which),
            [((16, 128, 256), BF, VMEM)],
            [SMEM, SMEM, VMEM, VMEM],
            [pltpu.VMEM((17, 128, 256), F32)],
            **heavy,
        )(lists, groups, tile, nodes)[0]
        for which in (1, 0)
    ]
    pair = (keep.astype(F32) + swap(send).astype(F32)).astype(BF)
    parts = exchange(pair, ("zh", "y"))
    output, spread = call(
        middle_kernel,
        [((128, 256), BF, VMEM), ((16, 320, 128), BF, VMEM)],
        [VMEM, VMEM, VMEM],
    )(parts, weight, cotangent)
    own = exchange(spread, ("zh", "y"))
    other = swap(own)
    (begun,) = call(
        backward_own_kernel,
        [((17, 256, 128), F32, VMEM)],
        [SMEM, SMEM, VMEM, VMEM],
        **heavy,
    )(lists, groups, tile, own)
    back, _ = call(
        backward_other_kernel,
        [((4, 1088, 128), BF, VMEM), ((17, 256, 128), F32, VMEM)],
        [SMEM, SMEM] + [VMEM] * 4,
        alias={5: 1},
        **heavy,
    )(lists, groups, tile, own, other, begun)
    folded = call(fold_kernel, [((320, 128), BF, VMEM)] * 4, [VMEM])(exchange(back, "x"))
    folded = [folded[0]] + [rotate(folded[k], "zl", k) for k in (1, 2, 3)]
    (grad,) = call(
        functools.partial(grad_kernel, 1.0 / math.sqrt(nodes_total)),
        [((8, 32, 256), BF, VMEM)],
        [SMEM] + [VMEM] * 4,
        [pltpu.VMEM((4, 64, 128), F32)],
    )(info, *folded)
    weight_grad = exchange(grad, "y").reshape(256, 256).astype(F32)
    (input_grad,) = call(last_kernel, [((128, 256), BF, VMEM)], [VMEM] * 5, flops=2**24, size=2**20)(*folded, weight)
    return (output, input_grad, weight_grad)


def solution(mesh):
    names = ("zl", "x", "zh", "y", "c")
    row, col = names[:2], names[2:]
    fine = Mesh(mesh.devices.reshape(4, 4, 2, 8, 2), names)
    return jax.shard_map(
        shards,
        mesh=fine,
        in_specs=(
            P(col + row, None),
            P(),
            P(row + col, None),
            P(row, col, None, None, None),
            P(row, col, None),
            P(row, col),
        ),
        out_specs=(P(row + col, None), P(col + row, None), P()),
        check_vma=False,
    )
```

```python
import functools
import math

import jax
import jax.numpy as jnp
from jax import lax
from jax.experimental import pallas as pl
from jax.experimental.pallas import tpu as pltpu
from jax.sharding import Mesh
from jax.sharding import PartitionSpec as P

BF = jnp.bfloat16
F32 = jnp.float32
GROUP = 16
SLOTS = 112
VMEM = pl.BlockSpec(memory_space=pltpu.VMEM)
SMEM = pl.BlockSpec(memory_space=pltpu.SMEM)
LIMIT = pltpu.CompilerParams(vmem_limit_bytes=48 * 1024 * 1024)


def dot(a, b, dims=(((1,), (0,)), ((), ()))):
    return lax.dot_general(a, b, dims, preferred_element_type=F32)


def plan_kernel(place, info, blocks, lists, groups):
    count, core = info[0], info[1]

    def write(at, k, t, source, half, target):
        for f, value in enumerate((k, t, source, half, target)):
            lists[f * 2 * SLOTS + at] = value

    def step(k, held):
        p = place[k]
        t, a = p >> 4, p & 15
        z, x = a >> 2, a & 3
        half = t >> 1
        source = (x << 2) + z
        target = (x << 2) + z
        mine, theirs = held
        away = (t & 1) ^ core
        write(jnp.where(away == 0, mine, SLOTS + theirs), k, half, source, half, target)
        return mine + 1 - away, theirs + away

    mine, theirs = lax.fori_loop(0, count, step, (jnp.int32(0), jnp.int32(0)))
    for i, n in enumerate((mine, theirs)):
        for g in range(GROUP):
            write(i * SLOTS + n + g, 0, 16, 0, 0, 16)
        groups[i] = (n + GROUP - 1) // GROUP


def entry(lists, which, field, j):
    return lists[field * 2 * SLOTS + which * SLOTS + j]


def forward_kernel(which, lists, groups, blocks, nodes, out, acc):
    acc[...] = jnp.zeros_like(acc)

    def step(i, _):
        products = []
        for g in range(GROUP):
            j = i * GROUP + g
            product = dot(blocks[entry(lists, which, 0, j)], nodes[entry(lists, which, 2, j)])
            products.append((entry(lists, which, 1, j), product))
        for slot, product in products:
            acc[slot] += product
        return 0

    lax.fori_loop(0, groups[which], step, 0)
    out[...] = acc[0:16].astype(BF)


def middle_kernel(parts, weight, cotangent, output, spread):
    total = parts[0].astype(F32)
    for s in range(1, 16):
        total += parts[s].astype(F32)
    share = total.astype(BF)
    pre = dot(share, weight[...])
    sigma = 1.0 / (1.0 + jnp.exp(-pre))
    output[...] = (pre * sigma).astype(BF)
    slope = sigma * (1.0 + pre * (1.0 - sigma))
    slopes32 = cotangent[...].astype(F32) * slope
    slopes = slopes32.astype(BF)
    turned = slopes.astype(F32).T.astype(BF)
    grad = dot(share.astype(F32).T.astype(BF), slopes).astype(BF)
    for s in range(16):
        spread[s, 0:256, :] = turned
        rows = slice(32 * (s % 8), 32 * (s % 8) + 32)
        spread[s, 256:288, :] = grad[rows, 0:128]
        spread[s, 288:320, :] = grad[rows, 128:256]


def back_products(which, lists, groups, blocks, source, acc):
    def step(i, _):
        products = []
        for g in range(GROUP):
            j = i * GROUP + g
            product = dot(source[entry(lists, which, 3, j), 0:256, :], blocks[entry(lists, which, 0, j)])
            products.append((entry(lists, which, 4, j), product))
        for slot, product in products:
            acc[slot] += product
        return 0

    lax.fori_loop(0, groups[which], step, 0)


def backward_own_kernel(lists, groups, blocks, own, acc):
    acc[...] = jnp.zeros_like(acc)
    back_products(0, lists, groups, blocks, own, acc)


def backward_other_kernel(lists, groups, blocks, own, other, begun, out, acc):
    back_products(1, lists, groups, blocks, other, acc)
    grad = jnp.zeros((64, 128), F32)
    for s in range(16):
        grad += own[s, 256:320, :].astype(F32) + other[s, 256:320, :].astype(F32)
    grad = grad.astype(BF)
    for x in range(4):
        for z in range(4):
            out[x, 256 * z : 256 * z + 256, :] = acc[4 * x + z].astype(BF)
        out[x, 1024:1088, :] = grad


def fold_kernel(parts, out):
    grad = parts[0, 1024:1088, :].astype(F32)
    for x in range(1, 4):
        grad += parts[x, 1024:1088, :].astype(F32)
    grad = grad.astype(BF)
    for z in range(4):
        rows = slice(256 * z, 256 * z + 256)
        total = parts[0, rows, :].astype(F32)
        for x in range(1, 4):
            total += parts[x, rows, :].astype(F32)
        out[z, 0:256, :] = total.astype(BF)
        out[z, 256:320, :] = grad


def grad_kernel(scale, parts, grad_out):
    grad = parts[0, 256:320, :].astype(F32)
    for z in range(1, 4):
        grad += parts[z, 256:320, :].astype(F32)
    grad = (grad * scale).astype(BF)
    for s in range(8):
        grad_out[s, :, 0:128] = grad[0:32]
        grad_out[s, :, 128:256] = grad[32:64]


def last_kernel(parts, weight, input_grad):
    total = parts[0, 0:256, :].astype(F32)
    for z in range(1, 4):
        total += parts[z, 0:256, :].astype(F32)
    back = total.astype(BF).astype(F32).T.astype(BF)
    input_grad[...] = dot(back, weight[...], (((1,), (1,)), ((), ()))).astype(BF)


def call(kernel, outs, kinds, scratch=(), flops=0, size=0, alias=None):
    return pl.pallas_call(
        kernel,
        out_shape=[jax.ShapeDtypeStruct(s, d) for s, d, _ in outs],
        in_specs=kinds,
        out_specs=[k for _, _, k in outs],
        scratch_shapes=list(scratch),
        input_output_aliases=alias or {},
        compiler_params=LIMIT,
        cost_estimate=pl.CostEstimate(flops=flops, bytes_accessed=size, transcendentals=0),
    )


def exchange(value, axes):
    return lax.all_to_all(value, axes, 0, 0, tiled=True)


def swap(value):
    return lax.ppermute(value, "c", [(0, 1), (1, 0)])


def shards(features, weight, cotangent, blocks, block_pos, counts):
    tile = blocks[0, 0]
    info = jnp.stack([counts[0, 0], lax.axis_index("c").astype(jnp.int32)])
    nodes_total = 65536
    heavy = dict(flops=8 * 10**8, size=6 * 2**20)
    i32 = jnp.int32

    lists, groups = call(
        plan_kernel,
        [((10 * SLOTS,), i32, SMEM), ((2,), i32, SMEM)],
        [SMEM, SMEM, VMEM],
        size=2**20,
    )(block_pos[0, 0], info, tile)

    line = exchange(jnp.broadcast_to(features[None], (4, 128, 256)), "zl")
    nodes = exchange(jnp.broadcast_to(line[None], (4, 4, 128, 256)), "x").reshape(16, 128, 256)
    send, keep = [
        call(
            functools.partial(forward_kernel, which),
            [((16, 128, 256), BF, VMEM)],
            [SMEM, SMEM, VMEM, VMEM],
            [pltpu.VMEM((17, 128, 256), F32)],
            **heavy,
        )(lists, groups, tile, nodes)[0]
        for which in (1, 0)
    ]
    pair = (keep.astype(F32) + swap(send).astype(F32)).astype(BF)
    parts = exchange(pair, ("zh", "y"))
    output, spread = call(
        middle_kernel,
        [((128, 256), BF, VMEM), ((16, 320, 128), BF, VMEM)],
        [VMEM, VMEM, VMEM],
    )(parts, weight, cotangent)
    own = exchange(spread, ("zh", "y"))
    other = swap(own)
    (begun,) = call(
        backward_own_kernel,
        [((17, 256, 128), F32, VMEM)],
        [SMEM, SMEM, VMEM, VMEM],
        **heavy,
    )(lists, groups, tile, own)
    back, _ = call(
        backward_other_kernel,
        [((4, 1088, 128), BF, VMEM), ((17, 256, 128), F32, VMEM)],
        [SMEM, SMEM] + [VMEM] * 4,
        alias={5: 1},
        **heavy,
    )(lists, groups, tile, own, other, begun)
    (folded,) = call(fold_kernel, [((4, 320, 128), BF, VMEM)], [VMEM])(exchange(back, "x"))
    folded = exchange(folded, "zl")
    scale = 1.0 / math.sqrt(nodes_total)
    (grad,) = call(functools.partial(grad_kernel, scale), [((8, 32, 256), BF, VMEM)], [VMEM])(folded)
    weight_grad = exchange(grad, "y").reshape(256, 256).astype(F32)
    (input_grad,) = call(last_kernel, [((128, 256), BF, VMEM)], [VMEM] * 2, flops=2**24, size=2**20)(folded, weight)
    return (output, input_grad, weight_grad)


def solution(mesh):
    names = ("zl", "x", "zh", "y", "c")
    row, col = names[:2], names[2:]
    fine = Mesh(mesh.devices.reshape(4, 4, 2, 8, 2), names)
    return jax.shard_map(
        shards,
        mesh=fine,
        in_specs=(
            P(col + row, None),
            P(),
            P(row + col, None),
            P(row, col, None, None, None),
            P(row, col, None),
            P(row, col),
        ),
        out_specs=(P(row + col, None), P(col + row, None), P()),
        check_vma=False,
    )
```

```python
import functools
import math

import jax
import jax.numpy as jnp
from jax import lax
from jax.experimental import pallas as pl
from jax.experimental.pallas import tpu as pltpu
from jax.sharding import Mesh
from jax.sharding import PartitionSpec as P

BF = jnp.bfloat16
F32 = jnp.float32
GROUP = 16
SLOTS = 112
VMEM = pl.BlockSpec(memory_space=pltpu.VMEM)
SMEM = pl.BlockSpec(memory_space=pltpu.SMEM)
LIMIT = pltpu.CompilerParams(vmem_limit_bytes=48 * 1024 * 1024)


def dot(a, b, dims=(((1,), (0,)), ((), ()))):
    return lax.dot_general(a, b, dims, preferred_element_type=F32)


def plan_kernel(place, info, blocks, lists, groups):
    count, core = info[0], info[1]

    def write(at, k, t, source, half, target):
        for f, value in enumerate((k, t, source, half, target)):
            lists[f * 2 * SLOTS + at] = value

    def step(k, held):
        p = place[k]
        t, a = p >> 4, p & 15
        z, x = a >> 2, a & 3
        half = t >> 1
        source = (x << 2) + z
        target = (x << 2) + z
        mine, theirs = held
        away = (t & 1) ^ core
        write(jnp.where(away == 0, mine, SLOTS + theirs), k, half, source, half, target)
        return mine + 1 - away, theirs + away

    mine, theirs = lax.fori_loop(0, count, step, (jnp.int32(0), jnp.int32(0)))
    for i, n in enumerate((mine, theirs)):
        for g in range(GROUP):
            write(i * SLOTS + n + g, 0, 16, 0, 0, 16)
        groups[i] = (n + GROUP - 1) // GROUP


def entry(lists, which, field, j):
    return lists[field * 2 * SLOTS + which * SLOTS + j]


def forward_kernel(which, lists, groups, blocks, nodes, out, acc):
    acc[...] = jnp.zeros_like(acc)

    def step(i, _):
        products = []
        for g in range(GROUP):
            j = i * GROUP + g
            product = dot(blocks[entry(lists, which, 0, j)], nodes[entry(lists, which, 2, j)])
            products.append((entry(lists, which, 1, j), product))
        for slot, product in products:
            acc[slot] += product
        return 0

    lax.fori_loop(0, groups[which], step, 0)
    out[...] = acc[0:16].astype(BF)


def middle_kernel(parts, weight, cotangent, output, spread):
    total = parts[0].astype(F32)
    for s in range(1, 16):
        total += parts[s].astype(F32)
    share = total.astype(BF)
    pre = dot(share, weight[...])
    sigma = 1.0 / (1.0 + jnp.exp(-pre))
    output[...] = (pre * sigma).astype(BF)
    slope = sigma * (1.0 + pre * (1.0 - sigma))
    slopes32 = cotangent[...].astype(F32) * slope
    slopes = slopes32.astype(BF)
    turned = slopes.astype(F32).T.astype(BF)
    columns = share.astype(F32).T.astype(BF)
    for s in range(16):
        spread[s, 0:256, :] = turned
        spread[s, 256:288, :] = columns[32 * (s % 8) : 32 * (s % 8) + 32]


def back_products(which, lists, groups, blocks, source, acc):
    def step(i, _):
        products = []
        for g in range(GROUP):
            j = i * GROUP + g
            product = dot(source[entry(lists, which, 3, j), 0:256, :], blocks[entry(lists, which, 0, j)])
            products.append((entry(lists, which, 4, j), product))
        for slot, product in products:
            acc[slot] += product
        return 0

    lax.fori_loop(0, groups[which], step, 0)


def chunk_sum(part):
    total = jnp.zeros((32, 256), F32)
    for s in range(16):
        total += dot(part[s, 256:288, :], part[s, 0:256, :], (((1,), (1,)), ((), ())))
    return total


def backward_own_kernel(lists, groups, blocks, own, acc, half):
    half[...] = chunk_sum(own)
    acc[...] = jnp.zeros_like(acc)
    back_products(0, lists, groups, blocks, own, acc)


def backward_other_kernel(lists, groups, blocks, other, half, begun, out, acc):
    back_products(1, lists, groups, blocks, other, acc)
    grad = (half[...] + chunk_sum(other)).astype(BF)
    for x in range(4):
        for z in range(4):
            out[x, 256 * z : 256 * z + 256, :] = acc[4 * x + z].astype(BF)
        out[x, 1024:1056, :] = grad[:, 0:128]
        out[x, 1056:1088, :] = grad[:, 128:256]


def fold_kernel(parts, out):
    grad = parts[0, 1024:1088, :].astype(F32)
    for x in range(1, 4):
        grad += parts[x, 1024:1088, :].astype(F32)
    grad = grad.astype(BF)
    for z in range(4):
        rows = slice(256 * z, 256 * z + 256)
        total = parts[0, rows, :].astype(F32)
        for x in range(1, 4):
            total += parts[x, rows, :].astype(F32)
        out[z, 0:256, :] = total.astype(BF)
        out[z, 256:320, :] = grad


def grad_kernel(scale, parts, grad_out):
    grad = parts[0, 256:320, :].astype(F32)
    for z in range(1, 4):
        grad += parts[z, 256:320, :].astype(F32)
    grad = (grad * scale).astype(BF)
    for s in range(8):
        grad_out[s, :, 0:128] = grad[0:32]
        grad_out[s, :, 128:256] = grad[32:64]


def last_kernel(parts, weight, input_grad):
    total = parts[0, 0:256, :].astype(F32)
    for z in range(1, 4):
        total += parts[z, 0:256, :].astype(F32)
    back = total.astype(BF).astype(F32).T.astype(BF)
    input_grad[...] = dot(back, weight[...], (((1,), (1,)), ((), ()))).astype(BF)


def call(kernel, outs, kinds, scratch=(), flops=0, size=0, alias=None):
    return pl.pallas_call(
        kernel,
        out_shape=[jax.ShapeDtypeStruct(s, d) for s, d, _ in outs],
        in_specs=kinds,
        out_specs=[k for _, _, k in outs],
        scratch_shapes=list(scratch),
        input_output_aliases=alias or {},
        compiler_params=LIMIT,
        cost_estimate=pl.CostEstimate(flops=flops, bytes_accessed=size, transcendentals=0),
    )


def exchange(value, axes):
    return lax.all_to_all(value, axes, 0, 0, tiled=True)


def swap(value):
    return lax.ppermute(value, "c", [(0, 1), (1, 0)])


def shards(features, weight, cotangent, blocks, block_pos, counts):
    tile = blocks[0, 0]
    info = jnp.stack([counts[0, 0], lax.axis_index("c").astype(jnp.int32)])
    nodes_total = 65536
    heavy = dict(flops=8 * 10**8, size=6 * 2**20)
    i32 = jnp.int32

    lists, groups = call(
        plan_kernel,
        [((10 * SLOTS,), i32, SMEM), ((2,), i32, SMEM)],
        [SMEM, SMEM, VMEM],
        size=2**20,
    )(block_pos[0, 0], info, tile)

    line = exchange(jnp.broadcast_to(features[None], (4, 128, 256)), "zl")
    nodes = exchange(jnp.broadcast_to(line[None], (4, 4, 128, 256)), "x").reshape(16, 128, 256)
    send, keep = [
        call(
            functools.partial(forward_kernel, which),
            [((16, 128, 256), BF, VMEM)],
            [SMEM, SMEM, VMEM, VMEM],
            [pltpu.VMEM((17, 128, 256), F32)],
            **heavy,
        )(lists, groups, tile, nodes)[0]
        for which in (1, 0)
    ]
    pair = (keep.astype(F32) + swap(send).astype(F32)).astype(BF)
    parts = exchange(pair, ("zh", "y"))
    output, spread = call(
        middle_kernel,
        [((128, 256), BF, VMEM), ((16, 288, 128), BF, VMEM)],
        [VMEM, VMEM, VMEM],
    )(parts, weight, cotangent)
    own = exchange(spread, ("zh", "y"))
    other = swap(own)
    begun, half = call(
        backward_own_kernel,
        [((17, 256, 128), F32, VMEM), ((32, 256), F32, VMEM)],
        [SMEM, SMEM, VMEM, VMEM],
        **heavy,
    )(lists, groups, tile, own)
    back, _ = call(
        backward_other_kernel,
        [((4, 1088, 128), BF, VMEM), ((17, 256, 128), F32, VMEM)],
        [SMEM, SMEM] + [VMEM] * 4,
        alias={5: 1},
        **heavy,
    )(lists, groups, tile, other, half, begun)
    (folded,) = call(fold_kernel, [((4, 320, 128), BF, VMEM)], [VMEM])(exchange(back, "x"))
    folded = exchange(folded, "zl")
    scale = 1.0 / math.sqrt(nodes_total)
    (grad,) = call(functools.partial(grad_kernel, scale), [((8, 32, 256), BF, VMEM)], [VMEM])(folded)
    weight_grad = exchange(grad, "y").reshape(256, 256).astype(F32)
    (input_grad,) = call(last_kernel, [((128, 256), BF, VMEM)], [VMEM] * 2, flops=2**24, size=2**20)(folded, weight)
    return (output, input_grad, weight_grad)


def solution(mesh):
    names = ("zl", "x", "zh", "y", "c")
    row, col = names[:2], names[2:]
    fine = Mesh(mesh.devices.reshape(4, 4, 2, 8, 2), names)
    return jax.shard_map(
        shards,
        mesh=fine,
        in_specs=(
            P(col + row, None),
            P(),
            P(row + col, None),
            P(row, col, None, None, None),
            P(row, col, None),
            P(row, col),
        ),
        out_specs=(P(row + col, None), P(col + row, None), P()),
        check_vma=False,
    )
```
